256 devices in a mesh: ctx: 32 (over y, x, core), tp: 8 (over z).
Axes of the slice: x: 4, y: 4, z: 8, core: 2. Of those that a mesh axis runs over, the one named last changes fastest.
Arguments:
- value: bfloat16 [8192, 8192], P('ctx', 'tp'), may hold values from -6 to 6
- gate_q1: bfloat16 [8192, 8192], P('ctx', 'tp'), may hold values from -6 to 6
- gate_k1: bfloat16 [8192, 8192], P('ctx', 'tp'), may hold values from -6 to 6
- gate_q2: bfloat16 [8192, 8192], P('ctx', 'tp'), may hold values from -6 to 6
- gate_k2: bfloat16 [8192, 8192], P('ctx', 'tp'), may hold values from -6 to 6
- gate_q3: bfloat16 [8192, 8192], P('ctx', 'tp'), may hold values from -6 to 6
- gate_k3: bfloat16 [8192, 8192], P('ctx', 'tp'), may hold values from -6 to 6
- grad_out: bfloat16 [8192, 8192], P('ctx', 'tp'), may hold values from -6 to 6
- short_filter: bfloat16 [7, 8192], P(None, 'tp'), may hold values from -2 to 2
- medium_filter: bfloat16 [128, 512], replicated, may hold values from -0.5 to 0.5
- residues: float32 [16, 512], replicated, may hold values from -1.5 to 1.5
- rates: float32 [16, 512], replicated, may hold values from 3e-05 to 0.05
Outputs:
- mixed: bfloat16 [8192, 8192], P('ctx', 'tp')
- grad_value: bfloat16 [8192, 8192], P('ctx', 'tp')
- grad_q1: bfloat16 [8192, 8192], P('ctx', 'tp')
- grad_k1: bfloat16 [8192, 8192], P('ctx', 'tp')
- grad_q2: bfloat16 [8192, 8192], P('ctx', 'tp')
- grad_k2: bfloat16 [8192, 8192], P('ctx', 'tp')
- grad_q3: bfloat16 [8192, 8192], P('ctx', 'tp')
- grad_k3: bfloat16 [8192, 8192], P('ctx', 'tp')
- grad_short: float32 [7, 8192], P(None, 'tp')
- grad_medium: float32 [128, 512], replicated
The draws below stay inside these ranges and needn't reach their ends.
All inputs are finite; a program needn't handle non-finite values.
Results may differ from the reference program's by a relative error of at most 0.02.
Values may be sent and summed in bfloat16 or wider, within the bound.
No kernel may reach another device: no remote copies, remote signals or barrier semaphores. Data moves between devices by JAX's collectives and lax.ppermute only.
A program may use at most 128 MiB of HBM per device.

```python
import math
import jax
import jax.numpy as jnp
from jax import lax

D = 8192
GROUPS = 512
SHORT = 7
MEDIUM = 128
MODES = 16
LENGTH = 8192


def steps_of(stream_key, dims, shards, low, largest):
    gain, own = 1.0, jax.random.fold_in(stream_key, 6)
    for position, parts in shards:
        draws = jnp.exp(jax.random.uniform(jax.random.fold_in(own, position), (parts,), jnp.float32, low / len(shards), largest / len(shards)))
        gain = gain * jnp.repeat(draws, dims[position] // parts).reshape([-1 if axis == position else 1 for axis in range(len(dims))])
    return gain


def noise(rng, shape, deviation, most, shards=(), kind=jnp.bfloat16):
    result = deviation * jax.random.normal(rng, shape, jnp.float32)
    if shards:
        result = result * steps_of(rng, shape, shards, -0.22, 0.18)
    return jnp.clip(result, -most, most).astype(kind)


def setup_inputs(seed: int = 0) -> dict:
    key_list = jax.random.split(jax.random.key(seed), 13)
    return {
        "value": noise(key_list[0], (LENGTH, D), 1.0, 6.0, ((0, 32), (1, 8))),
        "gate_q1": noise(key_list[1], (LENGTH, D), 1.0, 6.0, ((0, 32), (1, 8))),
        "gate_k1": noise(key_list[2], (LENGTH, D), 1.0, 6.0, ((0, 32), (1, 8))),
        "gate_q2": noise(key_list[3], (LENGTH, D), 1.0, 6.0, ((0, 32), (1, 8))),
        "gate_k2": noise(key_list[4], (LENGTH, D), 1.0, 6.0, ((0, 32), (1, 8))),
        "gate_q3": noise(key_list[5], (LENGTH, D), 1.0, 6.0, ((0, 32), (1, 8))),
        "gate_k3": noise(key_list[6], (LENGTH, D), 1.0, 6.0, ((0, 32), (1, 8))),
        "grad_out": noise(key_list[7], (LENGTH, D), 1.0, 6.0, ((0, 32), (1, 8))),
        "short_filter": noise(key_list[8], (SHORT, D), SHORT ** -0.5, 2.0, ((1, 8),)),
        "medium_filter": noise(key_list[9], (MEDIUM, GROUPS), MEDIUM ** -0.5, 0.5),
        "residues": noise(key_list[10], (MODES, GROUPS), 0.25, 1.5, (), jnp.float32),
        "rates": jnp.clip(jnp.exp(jax.random.uniform(key_list[11], (MODES, GROUPS), jnp.float32, math.log(2.9999999242136255e-05), math.log(0.05))), 2.9999999242136255e-05, 0.05),
    }


def causal(signal, filt):
    size = 2 * signal.shape[0]
    spec = jnp.fft.rfft(signal, n=size, axis=0) * jnp.fft.rfft(filt, n=size, axis=0)
    return jnp.fft.irfft(spec, n=size, axis=0)[:signal.shape[0]]

def adjoint(signal, filt):
    return causal(signal[::-1], filt)[::-1]

def lagged(grads, signal, taps):
    size = 2 * signal.shape[0]
    spec = jnp.fft.rfft(grads, n=size, axis=0) * jnp.conj(jnp.fft.rfft(signal, n=size, axis=0))
    return jnp.fft.irfft(spec, n=size, axis=0)[:taps]

def reference(value, gate_q1, gate_k1, gate_q2, gate_k2, gate_q3, gate_k3, grad_out, short_filter, medium_filter, residues, rates):
    f32 = jnp.float32
    bf = jnp.bfloat16
    copies = D // GROUPS
    med = jnp.tile(medium_filter.astype(f32), (1, copies))
    weight = residues * jnp.sqrt(2.0 * rates)
    steps_n = jnp.arange(LENGTH).astype(f32)[:, None]
    longf = jnp.zeros((LENGTH, GROUPS), f32)
    for mode in range(MODES):
        longf = longf + weight[mode][None, :] * jnp.exp(-rates[mode][None, :] * steps_n)
    longf = jnp.tile(longf, (1, copies))
    shortf = short_filter.astype(f32)

    def mul(a, b):
        return a.astype(f32) * b.astype(f32)
    u1 = mul(gate_k1, value).astype(bf)
    z1 = causal(u1.astype(f32), shortf)
    x1 = mul(gate_q1, z1).astype(bf)
    u2 = mul(gate_k2, x1).astype(bf)
    z2 = causal(u2.astype(f32), med)
    x2 = mul(gate_q2, z2).astype(bf)
    u3 = mul(gate_k3, x2).astype(bf)
    z3 = causal(u3.astype(f32), longf)
    mixed = mul(gate_q3, z3).astype(bf)
    grad_q3 = mul(grad_out, z3).astype(bf)
    dz3 = mul(grad_out, gate_q3)
    du3 = adjoint(dz3, longf)
    grad_k3 = mul(du3, x2).astype(bf)
    dx2 = mul(du3, gate_k3).astype(bf)
    grad_q2 = mul(dx2, z2).astype(bf)
    dz2 = mul(dx2, gate_q2).astype(bf)
    du2 = adjoint(dz2.astype(f32), med)
    grad_k2 = mul(du2, x1).astype(bf)
    dx1 = mul(du2, gate_k2).astype(bf)
    grad_q1 = mul(dx1, z1).astype(bf)
    dz1 = mul(dx1, gate_q1).astype(bf)
    du1 = adjoint(dz1.astype(f32), shortf)
    grad_k1 = mul(du1, value).astype(bf)
    grad_value = mul(du1, gate_k1).astype(bf)
    grad_short = lagged(dz1.astype(f32), u1.astype(f32), SHORT)
    grad_wide = lagged(dz2.astype(f32), u2.astype(f32), MEDIUM)
    grad_medium = lax.optimization_barrier(jnp.sum(grad_wide.reshape(MEDIUM, copies, GROUPS), axis=1))
    return (mixed, grad_value, grad_q1, grad_k1, grad_q2, grad_k2, grad_q3, grad_k3, grad_short, grad_medium)
```

```python
import functools

import jax
import jax.numpy as jnp
import numpy as np
from jax import lax
from jax.experimental import pallas as pl
from jax.experimental.pallas import tpu as pltpu
from jax.sharding import PartitionSpec as P

F32 = jnp.float32
BF = jnp.bfloat16
LANES = 128
VMEM_LIMIT = 40 * 1024 * 1024


def dft_tables(count):
    size = 2 * count
    freq = np.arange(count)[:, None].astype(np.int64)

    def waves(times):
        phase = (freq * times[None, :]) % size * (2.0 * np.pi / size)
        cosine, sine = np.cos(phase), -np.sin(phase)
        sine[0] = np.where(times % 2 == 0, 1.0, -1.0)
        return np.concatenate([cosine, sine], axis=0)

    forward = waves(np.arange(size))
    scale = np.full((size, 1), 2.0 / size)
    scale[0] = scale[count] = 1.0 / size
    backward = (forward * scale).T
    return forward, backward


def dot(a, b):
    return jnp.dot(a, b, preferred_element_type=F32)


def spec_mul(spec, filt):
    half = spec.shape[0] // 2
    re, im = spec[:half], spec[half:]
    a, b, c = filt
    return jnp.concatenate([(re * a - im * b).astype(BF), (re * b + im * c).astype(BF)], axis=0)


def spec_conj(spec, filt):
    half = spec.shape[0] // 2
    re, im = spec[:half], spec[half:]
    a, b, c = filt
    return jnp.concatenate([(re * a + im * b).astype(BF), (im * c - re * b).astype(BF)], axis=0)


def row_index(shape):
    return lax.broadcasted_iota(jnp.int32, shape, 0)


def end_states(signal_ref, rates_ref, out_ref, reverse):
    count, width = signal_ref.shape
    modes = rates_ref.shape[0]
    tiles = count // 8
    for group in range(width // LANES):
        lanes = slice(group * LANES, (group + 1) * LANES)
        rates = rates_ref[:, lanes]
        step = jnp.exp(-8.0 * rates)
        steps = [jnp.broadcast_to(step[m : m + 1], (8, LANES)) for m in range(modes)]

        def body(j, sums, lanes=lanes, steps=steps):
            tile = tiles - 1 - j if reverse else j
            u = signal_ref[pl.ds(pl.multiple_of(tile * 8, 8), 8), lanes]
            return tuple(s * a + u for s, a in zip(sums, steps))

        zero = jnp.zeros((8, LANES), F32)
        sums = lax.fori_loop(0, tiles, body, (zero,) * modes, unroll=4)
        sub = row_index((8, LANES)).astype(F32)
        ages = sub if reverse else 7.0 - sub
        rows = [
            jnp.sum(s * jnp.exp(-rates[m : m + 1] * ages), axis=0, keepdims=True)
            for m, s in enumerate(sums)
        ]
        out_ref[:, lanes] = jnp.concatenate(rows, axis=0)


def far_field(states, rates_ref, weights_ref, out_ref, reverse, first, lanes):
    count = out_ref.shape[0]
    modes = rates_ref.shape[0]
    tiles = count // 8
    rates = rates_ref[:, lanes]
    weights = weights_ref[:, lanes] * jnp.sqrt(2.0 * rates)
    if states is not None:
        weights = weights * states
    step = jnp.exp(-8.0 * rates)
    steps = [jnp.broadcast_to(step[m : m + 1], (8, LANES)) for m in range(modes)]
    sub = row_index((8, LANES)).astype(F32)
    ages = (7.0 - sub if reverse else sub) + float(first)
    terms = tuple(weights[m : m + 1] * jnp.exp(-rates[m : m + 1] * ages) for m in range(modes))

    def body(j, terms):
        tile = tiles - 1 - j if reverse else j
        level = list(terms)
        while len(level) > 1:
            level = [level[i] + level[i + 1] for i in range(0, len(level), 2)]
        out_ref[pl.ds(pl.multiple_of(tile * 8, 8), 8), lanes] = level[0]
        return tuple(s * a for s, a in zip(terms, steps))

    lax.fori_loop(0, tiles, body, terms, unroll=4)


def add_far(state_ref, rates_ref, weights_ref, out_ref, reverse):
    for group in range(out_ref.shape[1] // LANES):
        lanes = slice(group * LANES, (group + 1) * LANES)
        far_field(state_ref[:, lanes], rates_ref, weights_ref, out_ref, reverse, 1, lanes)


def mul(a, b):
    return a.astype(F32) * b.astype(F32)


def back_carry_kernel(grad_ref, gate_ref, rates_ref, out_ref, signal):
    signal[...] = mul(grad_ref[...], gate_ref[...])
    end_states(signal, rates_ref, out_ref, True)


def short_causal(ext, filt_ref, rows, start):
    total = None
    for lag in range(filt_ref.shape[0]):
        term = ext[pl.ds(start - lag, rows), :] * filt_ref[lag : lag + 1, :].astype(F32)
        total = term if total is None else total + term
    return total


def fore_rim_kernel(value_ref, k1_ref, q1_ref, k2_ref, filt_ref, out_ref, ext):
    count = value_ref.shape[0]
    rim = q1_ref.shape[0]
    u1 = mul(k1_ref[...], value_ref[...]).astype(BF)
    ext[...] = u1.astype(F32)
    z1 = short_causal(ext, filt_ref, rim, count - rim)
    x1 = mul(q1_ref[...], z1).astype(BF)
    out_ref[0:rim, :] = mul(k2_ref[...], x1).astype(BF)
    out_ref[rim : rim + 16, :] = u1[count - 16 :]


def filters_kernel(table_ref, medium_ref, residues_ref, rates_ref, ma, mb, mc, la, lb, lc, local):
    highest = lax.Precision.HIGHEST
    count = local.shape[0]
    taps = medium_ref.shape[0]
    for group in range(local.shape[1] // LANES):
        lanes = slice(group * LANES, (group + 1) * LANES)
        far_field(None, rates_ref, residues_ref, local, False, 0, lanes)
    table = table_ref[...]
    for filt, (a, b, c) in (
        (medium_ref[...].astype(F32), (ma, mb, mc)),
        (local[...], (la, lb, lc)),
    ):
        spec = jnp.dot(
            table[:, : filt.shape[0]], filt, precision=highest, preferred_element_type=F32
        )
        re, im = spec[:count], spec[count:]
        edge = row_index(re.shape) == 0
        a[...] = re
        b[...] = jnp.where(edge, 0.0, im)
        c[...] = jnp.where(edge, im, re)


def fore_kernel(
    value_ref, k1_ref, q1_ref, k2_ref, q2_ref, k3_ref, rim_ref, filt_ref, rates_ref,
    fwd_ref, inv_ref, ma, mb, mc,
    z1_ref, x1_ref, u2_ref, z2_ref, x2_ref, u3_ref, carry_ref, ext,
):
    count = value_ref.shape[0]
    rim = rim_ref.shape[0] - 16
    u1 = mul(k1_ref[...], value_ref[...]).astype(BF)
    ext[0:16, :] = rim_ref[rim : rim + 16, :].astype(F32)
    ext[16:, :] = u1.astype(F32)
    z1 = short_causal(ext, filt_ref, count, 16)
    z1_ref[...] = z1.astype(BF)
    x1 = mul(q1_ref[...], z1).astype(BF)
    x1_ref[...] = x1
    u2 = mul(k2_ref[...], x1).astype(BF)
    u2_ref[...] = u2
    spec = dot(fwd_ref[:, :count], u2) + dot(fwd_ref[:, 2 * count - rim :], rim_ref[0:rim, :])
    z2 = dot(inv_ref[...], spec_mul(spec, (ma[...], mb[...], mc[...])))
    z2_ref[...] = z2.astype(BF)
    x2 = mul(q2_ref[...], z2).astype(BF)
    x2_ref[...] = x2
    u3 = mul(k3_ref[...], x2).astype(BF)
    u3_ref[...] = u3
    ext[0:count, :] = u3.astype(F32)
    end_states(ext.at[0:count, :], rates_ref, carry_ref, False)


def back_local_kernel(grad_ref, gate_ref, fwd_ref, inv_ref, la, lb, lc, out_ref):
    count = grad_ref.shape[0]
    spec = dot(fwd_ref[:, :count], mul(grad_ref[...], gate_ref[...]).astype(BF))
    out_ref[...] = dot(inv_ref[...], spec_conj(spec, (la[...], lb[...], lc[...])))


def back_long_kernel(
    near_ref, state_ref, rates_ref, residues_ref, x2_ref, z2_ref, k3_ref, q2_ref, k2_ref, q1_ref,
    fwd_ref, inv_ref, ma, mb, mc,
    gk3_ref, gq2_ref, dz2_ref, du2_ref, rim_ref, far,
):
    count = near_ref.shape[0]
    rim = rim_ref.shape[0] - 16
    add_far(state_ref, rates_ref, residues_ref, far, True)
    du3 = near_ref[...] + far[...]
    gk3_ref[...] = mul(du3, x2_ref[...]).astype(BF)
    dx2 = mul(du3, k3_ref[...]).astype(BF)
    gq2_ref[...] = mul(dx2, z2_ref[...]).astype(BF)
    dz2 = mul(dx2, q2_ref[...]).astype(BF)
    dz2_ref[...] = dz2
    spec = dot(fwd_ref[:, :count], dz2)
    du2 = dot(inv_ref[...], spec_conj(spec, (ma[...], mb[...], mc[...])))
    du2_ref[...] = du2
    rim_ref[0:rim, :] = dz2[0:rim]
    dx1 = mul(du2[0:16], k2_ref[0:16, :]).astype(BF)
    rim_ref[rim : rim + 16, :] = mul(dx1, q1_ref[0:16, :]).astype(BF)


def medium_terms_kernel(dz2_ref, u2_ref, rim_ref, fwd_ref, lag_ref, out_ref, total):
    count = dz2_ref.shape[0]
    rim = rim_ref.shape[0]
    step = pl.program_id(0)
    ext = dot(fwd_ref[:, :count], u2_ref[...]) + dot(fwd_ref[:, 2 * count - rim :], rim_ref[...])
    grad = dot(fwd_ref[:, :count], dz2_ref[...])
    er, ei, dr, di = ext[:count], ext[count:], grad[:count], grad[count:]
    edge = row_index(er.shape) == 0
    high = di * ei
    re = dr * er + jnp.where(edge, 0.0, high)
    im = jnp.where(edge, high, dr * ei - di * er)
    cross = jnp.concatenate([re, im], axis=0)

    @pl.when(step % 2 == 0)
    def _():
        total[...] = cross

    @pl.when(step % 2 == 1)
    def _():
        out_ref[...] = dot(lag_ref[...], (total[...] + cross).astype(BF))


def back_short_kernel(
    du2_ref, rim_ref, x1_ref, z1_ref, k2_ref, q1_ref, k1_ref, value_ref, fore_ref, filt_ref,
    terms_ref, fwd_ref, inv_ref, ma, mb, mc,
    gk2_ref, gq1_ref, gk1_ref, gv_ref, send_ref, ext, signal,
):
    count = du2_ref.shape[0]
    rim = rim_ref.shape[0] - 16
    taps = filt_ref.shape[0]
    step = pl.program_id(0)
    spec = dot(fwd_ref[:, count : count + rim], rim_ref[0:rim, :])
    du2 = du2_ref[...] + dot(inv_ref[...], spec_conj(spec, (ma[...], mb[...], mc[...])))
    gk2_ref[...] = mul(du2, x1_ref[...]).astype(BF)
    dx1 = mul(du2, k2_ref[...]).astype(BF)
    gq1_ref[...] = mul(dx1, z1_ref[...]).astype(BF)
    dz1 = mul(dx1, q1_ref[...]).astype(BF).astype(F32)
    ext[0:count, :] = dz1
    ext[count:, :] = rim_ref[rim : rim + 16, :].astype(F32)
    signal[0:16, :] = fore_ref[...].astype(F32)
    signal[16:, :] = mul(k1_ref[...], value_ref[...]).astype(BF).astype(F32)
    du1 = None
    for lag in range(taps):
        term = ext[pl.ds(lag, count), :] * filt_ref[lag : lag + 1, :].astype(F32)
        du1 = term if du1 is None else du1 + term
    gk1_ref[...] = mul(du1, value_ref[...]).astype(BF)
    gv_ref[...] = mul(du1, k1_ref[...]).astype(BF)

    pieces, width = send_ref.shape[0], du2_ref.shape[1]

    @pl.when(step == 0)
    def _():
        send_ref[...] = jnp.zeros_like(send_ref)
        share = terms_ref.shape[0] // pieces
        half = terms_ref.shape[1] // 2
        for piece in range(pieces):
            rows = terms_ref[piece * share : (piece + 1) * share, :]
            send_ref[piece, 0:share, 0:half] = rows[:, :half]
            send_ref[piece, share : 2 * share, 0:half] = rows[:, half:]

    block = (step % 2) * 2 + step // 2
    for lag in range(taps):
        row = jnp.sum(dz1 * signal[pl.ds(16 - lag, count), :], axis=0, keepdims=True)
        spot = lag * 4 + block
        send_ref[spot, 0:1, width : width + LANES] = row[:, :LANES]
        send_ref[spot, 1:2, width : width + LANES] = row[:, LANES:]


def fore_long_kernel(
    u3_ref, state_ref, rates_ref, residues_ref, q3_ref, grad_ref, fwd_ref, inv_ref, la, lb, lc,
    mixed_ref, gq3_ref, far,
):
    count = u3_ref.shape[0]
    add_far(state_ref, rates_ref, residues_ref, far, False)
    spec = dot(fwd_ref[:, :count], u3_ref[...])
    z3 = far[...] + dot(inv_ref[...], spec_mul(spec, (la[...], lb[...], lc[...])))
    mixed_ref[...] = mul(q3_ref[...], z3).astype(BF)
    gq3_ref[...] = mul(grad_ref[...], z3).astype(BF)


def swapped(block, distance):
    size = lax.axis_size("ctx")
    return lax.ppermute(block, "ctx", [(i, i ^ distance) for i in range(size)])


def shifted(block, distance):
    size = lax.axis_size("ctx")
    route = [(i, i + distance) for i in range(size) if 0 <= i + distance < size]
    return lax.ppermute(block, "ctx", route)


def scan_states(carry, rates, count, reverse):
    size = lax.axis_size("ctx")
    place = lax.axis_index("ctx")
    if reverse:
        place = size - 1 - place
    drop = rates * float(-count)

    def power(n):
        return jnp.exp(drop * n.astype(F32))

    total, prefix = carry, jnp.zeros_like(carry)
    group = 1
    for fan in (2, 4, 4):
        mine = (place // group) % fan
        offset = place % group
        others = [(d, swapped(total, d * group)) for d in range(1, fan)]
        if group * fan < size:
            new_total = total * power(group * (fan - 1 - mine))
        for d, other in others:
            theirs = mine ^ d
            before = theirs < mine
            gap = jnp.where(before, offset + group * (mine - 1 - theirs), 0)
            prefix = prefix + jnp.where(before, power(gap), 0.0) * other
            if group * fan < size:
                new_total = new_total + power(group * (fan - 1 - theirs)) * other
        if group * fan < size:
            total = new_total
        group *= fan
    return prefix


def on_device(
    value, gate_q1, gate_k1, gate_q2, gate_k2, gate_q3, gate_k3, grad_out,
    short_filter, medium_filter, residues, rates,
):
    count, width = value.shape
    modes, groups = rates.shape
    copies = width // groups
    taps, medium_taps = short_filter.shape[0], medium_filter.shape[0]
    cb = groups // 2
    steps = copies * 2
    rim = medium_taps
    forward, backward = dft_tables(count)
    fwd32 = jnp.asarray(forward[:, :count], F32)
    fwd = jnp.asarray(forward, BF)
    inv = jnp.asarray(backward[:count], BF)
    lag = jnp.asarray(backward[(-np.arange(medium_taps)) % (2 * count)], BF)

    def chan(i):
        return (i % copies) * 2 + i // copies

    def data(rows, at=0):
        return pl.BlockSpec((rows, cb), lambda i: (at, chan(i)))

    def filt(rows):
        return pl.BlockSpec((rows, cb), lambda i: (0, i // copies))

    def whole(shape):
        return pl.BlockSpec(shape, lambda i: (0,) * len(shape))

    def shape(rows, dtype=BF, cols=width):
        return jax.ShapeDtypeStruct((rows, cols), dtype)

    def call(kernel, name, in_specs, out_specs, out_shape, scratch=()):
        return pl.pallas_call(
            kernel,
            name=name,
            grid=(steps,),
            in_specs=in_specs,
            out_specs=out_specs,
            out_shape=out_shape,
            scratch_shapes=list(scratch),
            compiler_params=pltpu.CompilerParams(vmem_limit_bytes=VMEM_LIMIT),
        )

    table_specs = [whole(fwd.shape), whole(inv.shape)]
    spec3 = [filt(count)] * 3
    wide_rates = jnp.tile(rates, (1, copies))

    back_carry = call(
        back_carry_kernel, "back_carry", [data(count)] * 2 + [filt(modes)], data(modes),
        shape(modes, F32), [pltpu.VMEM((count, cb), F32)],
    )(grad_out, gate_q3, rates)
    back_state = scan_states(back_carry, wide_rates, count, True)

    rim_send = call(
        fore_rim_kernel, "fore_rim",
        [data(count)] * 2 + [data(rim, 1)] * 2 + [data(taps)],
        data(rim + 16), shape(rim + 16), [pltpu.VMEM((count, cb), F32)],
    )(value, gate_k1, gate_q1, gate_k2, short_filter)
    rim_fore = shifted(rim_send, 1)

    spectra = pl.pallas_call(
        filters_kernel,
        name="filters",
        out_shape=[shape(count, F32, groups)] * 6,
        scratch_shapes=[pltpu.VMEM((count, groups), F32)],
        compiler_params=pltpu.CompilerParams(vmem_limit_bytes=VMEM_LIMIT),
    )(fwd32, medium_filter, residues, rates)
    med, lng = spectra[:3], spectra[3:]

    du3_near = call(
        back_local_kernel, "back_local", [data(count)] * 2 + table_specs + spec3, data(count),
        shape(count, F32),
    )(grad_out, gate_q3, fwd, inv, *lng)

    z1, x1, u2, z2, x2, u3, fore_carry = call(
        fore_kernel, "fore",
        [data(count)] * 6 + [data(rim + 16), data(taps), filt(modes)] + table_specs + spec3,
        [data(count)] * 6 + [data(modes)],
        [shape(count)] * 6 + [shape(modes, F32)],
        [pltpu.VMEM((count + 16, cb), F32)],
    )(value, gate_k1, gate_q1, gate_k2, gate_q2, gate_k3, rim_fore, short_filter, rates, fwd, inv, *med)
    fore_state = scan_states(fore_carry, wide_rates, count, False)

    grad_k3, grad_q2, dz2, du2_near, rim_back_send = call(
        back_long_kernel, "back_long",
        [data(count), data(modes), filt(modes), filt(modes)]
        + [data(count)] * 4 + [data(16)] * 2 + table_specs + spec3,
        [data(count)] * 4 + [data(rim + 16)],
        [shape(count)] * 3 + [shape(count, F32), shape(rim + 16)],
        [pltpu.VMEM((count, cb), F32)],
    )(du3_near, back_state, rates, residues, x2, z2, gate_k3, gate_q2, gate_k2, gate_q1, fwd, inv, *med)
    rim_back = shifted(rim_back_send, -1)

    terms = call(
        medium_terms_kernel, "medium_terms",
        [data(count)] * 2 + [data(rim)] + [whole(fwd.shape), whole(lag.shape)],
        filt(medium_taps), shape(medium_taps, F32, groups), [pltpu.VMEM((2 * count, cb), F32)],
    )(dz2, u2, rim_fore, fwd, lag)

    mixed, grad_q3 = call(
        fore_long_kernel, "fore_long",
        [data(count), data(modes), filt(modes), filt(modes)] + [data(count)] * 2 + table_specs + spec3,
        [data(count)] * 2, [shape(count)] * 2, [pltpu.VMEM((count, cb), F32)],
    )(u3, fore_state, rates, residues, gate_q3, grad_out, fwd, inv, *lng)

    ctx, tp = lax.axis_size("ctx"), lax.axis_size("tp")
    packet = (ctx, 8, cb + LANES)
    grad_k2, grad_q1, grad_k1, grad_value, send = call(
        back_short_kernel, "back_short",
        [data(count), data(rim + 16)] + [data(count)] * 6 + [data(16, rim // 16), data(taps)]
        + [whole((medium_taps, groups))] + table_specs + spec3,
        [data(count)] * 4 + [whole(packet)],
        [shape(count)] * 4 + [jax.ShapeDtypeStruct(packet, F32)],
        [pltpu.VMEM((count + 16, cb), F32)] * 2,
    )(du2_near, rim_back, x1, z1, gate_k2, gate_q1, gate_k1, value, rim_fore, short_filter, terms,
      fwd, inv, *med)

    got = lax.all_to_all(send, "ctx", 0, 0)
    part = jnp.sum(got, axis=0)
    spread = jnp.broadcast_to(part[None, :, :cb], (tp, 8, cb))
    medium = jnp.sum(lax.all_to_all(spread, "tp", 0, 0), axis=0)
    piece = jnp.concatenate([medium, part[:, cb:]], axis=1)
    full = lax.all_to_all(jnp.broadcast_to(piece[None], packet), "ctx", 0, 0)
    share = medium_taps // ctx
    grad_medium = (
        full[:, :, :cb].reshape(ctx, 2, share, cb).transpose(0, 2, 1, 3).reshape(medium_taps, groups)
    )
    grad_short = full[:, 0:2, cb:].reshape(8, width)[:taps]
    return (
        mixed, grad_value, grad_q1, grad_k1, grad_q2, grad_k2, grad_q3, grad_k3, grad_short, grad_medium,
    )


def solution(mesh):
    data = P("ctx", "tp")
    return jax.shard_map(
        on_device,
        mesh=mesh,
        in_specs=(data,) * 8 + (P(None, "tp"), P(), P(), P()),
        out_specs=(data,) * 8 + (P(None, "tp"), P()),
        check_vma=False,
    )
```

```python
import jax
import jax.numpy as jnp
import numpy as np
from jax import lax
from jax.experimental import pallas as pl
from jax.experimental.pallas import tpu as pltpu
from jax.sharding import PartitionSpec as P

F32 = jnp.float32
BF = jnp.bfloat16
LANES = 128
VMEM_LIMIT = 28 * 1024 * 1024
BLOCK = 256
UNROLL = 4


def dft_tables(count):
    size = 2 * count
    freq = np.arange(count)[:, None].astype(np.int64)

    def waves(times):
        phase = (freq * times[None, :]) % size * (2.0 * np.pi / size)
        cosine, sine = np.cos(phase), -np.sin(phase)
        sine[0] = np.where(times % 2 == 0, 1.0, -1.0)
        return np.concatenate([cosine, sine], axis=0)

    forward = waves(np.arange(size))
    scale = np.full((size, 1), 2.0 / size)
    scale[0] = scale[count] = 1.0 / size
    backward = (forward * scale).T
    return forward, backward


def dot(a, b):
    return jnp.dot(a, b, preferred_element_type=F32)


def spec_mul(spec, filt):
    half = spec.shape[0] // 2
    re, im = spec[:half], spec[half:]
    a, b, c = filt
    return jnp.concatenate([(re * a - im * b).astype(BF), (re * b + im * c).astype(BF)], axis=0)


def spec_conj(spec, filt):
    half = spec.shape[0] // 2
    re, im = spec[:half], spec[half:]
    a, b, c = filt
    return jnp.concatenate([(re * a + im * b).astype(BF), (im * c - re * b).astype(BF)], axis=0)


def row_index(shape):
    return lax.broadcasted_iota(jnp.int32, shape, 0)


def end_states(signal_ref, rates_ref, lanes, own, reverse):
    tiles = signal_ref.shape[0] // 8
    modes = rates_ref.shape[0]
    rates = rates_ref[:, own]
    step = jnp.exp(-8.0 * rates)
    steps = [jnp.broadcast_to(step[m : m + 1], (8, LANES)) for m in range(modes)]

    def body(j, sums):
        tile = tiles - 1 - j if reverse else j
        u = signal_ref[pl.ds(pl.multiple_of(tile * 8, 8), 8), lanes]
        return tuple(s * a + u for s, a in zip(sums, steps))

    zero = jnp.zeros((8, LANES), F32)
    sums = lax.fori_loop(0, tiles, body, (zero,) * modes, unroll=UNROLL)
    sub = row_index((8, LANES)).astype(F32)
    ages = sub if reverse else 7.0 - sub
    rows = [
        jnp.sum(s * jnp.exp(-rates[m : m + 1] * ages), axis=0, keepdims=True)
        for m, s in enumerate(sums)
    ]
    return jnp.concatenate(rows, axis=0)


def far_field(states, rates, weights, out_ref, reverse, first, lanes):
    tiles = out_ref.shape[0] // 8
    modes = rates.shape[0]
    weights = weights * jnp.sqrt(2.0 * rates)
    if states is not None:
        weights = weights * states
    step = jnp.exp(-8.0 * rates)
    steps = [jnp.broadcast_to(step[m : m + 1], (8, LANES)) for m in range(modes)]
    sub = row_index((8, LANES)).astype(F32)
    ages = (7.0 - sub if reverse else sub) + float(first)
    terms = tuple(weights[m : m + 1] * jnp.exp(-rates[m : m + 1] * ages) for m in range(modes))

    def body(j, terms):
        tile = tiles - 1 - j if reverse else j
        level = list(terms)
        while len(level) > 1:
            level = [level[i] + level[i + 1] for i in range(0, len(level), 2)]
        out_ref[pl.ds(pl.multiple_of(tile * 8, 8), 8), lanes] = level[0]
        return tuple(s * a for s, a in zip(terms, steps))

    lax.fori_loop(0, tiles, body, terms, unroll=UNROLL)


def parts(width, groups, size=BLOCK):
    for start in range(0, width, size):
        own = start % groups
        yield slice(start, start + size), slice(own, own + size)


def mul(a, b):
    return a.astype(F32) * b.astype(F32)


def short_causal(ext, filt, rows, start, lanes):
    total = None
    for lag in range(filt.shape[0]):
        term = ext[pl.ds(start - lag, rows), lanes] * filt[lag : lag + 1, lanes].astype(F32)
        total = term if total is None else total + term
    return total


def fore_rim_kernel(flow, place_ref, value_ref, k1_ref, q1_ref, k2_ref, filt_ref, out_ref, ext):
    del place_ref
    count, width = value_ref.shape
    rim = out_ref.shape[0] - 16
    top = count - rim - 16
    for block, (lanes, _) in enumerate(parts(width, width)):
        flow.ready(block)
        u1 = mul(k1_ref[top:, lanes], value_ref[top:, lanes]).astype(BF)
        ext[:, lanes] = u1.astype(F32)
        z1 = short_causal(ext, filt_ref, rim, 16, lanes)
        x1 = mul(q1_ref[count - rim :, lanes], z1).astype(BF)
        out_ref[0:rim, lanes] = mul(k2_ref[count - rim :, lanes], x1).astype(BF)
        out_ref[rim : rim + 16, lanes] = u1[rim:]


def spectrum(table, filt, out):
    count = out.shape[1]
    spec = jnp.dot(
        table[:, : filt.shape[0]], filt, precision=lax.Precision.HIGHEST, preferred_element_type=F32
    )
    re, im = spec[:count], spec[count:]
    edge = row_index(re.shape) == 0
    out[0] = re
    out[1] = jnp.where(edge, 0.0, im)
    out[2] = jnp.where(edge, im, re)


def medium_filter_kernel(flow, table_ref, medium_ref, *refs):
    out_ref = refs[-1]
    flow.ready(0)
    spectrum(table_ref, medium_ref[...].astype(F32), out_ref)
    for piece in range(1, 4):
        flow.ready(piece)


def long_filter_kernel(table_ref, residues_ref, rates_ref, out_ref, local):
    for lanes, _ in parts(local.shape[1], local.shape[1], LANES):
        far_field(None, rates_ref[:, lanes], residues_ref[:, lanes], local, False, 0, lanes)
    spectrum(table_ref, local[...], out_ref)


def filt_of(ref, own):
    return ref[0, :, own], ref[1, :, own], ref[2, :, own]


def back_carry_kernel(grad_ref, gate_ref, rates_ref, carry_ref, signal):
    count, width = grad_ref.shape
    groups = rates_ref.shape[1]
    for lanes, own in parts(width, groups):
        signal[:, lanes] = mul(grad_ref[:, lanes], gate_ref[:, lanes])
        for side in range(0, BLOCK, LANES):
            at = slice(lanes.start + side, lanes.start + side + LANES)
            mine = slice(own.start + side, own.start + side + LANES)
            carry_ref[:, at] = end_states(signal, rates_ref, at, mine, True)


def back_near_kernel(grad_ref, gate_ref, fwd_ref, inv_ref, long_ref, near_ref):
    count, width = grad_ref.shape
    for lanes, own in parts(width, long_ref.shape[2]):
        spec = dot(fwd_ref[:, :count], mul(grad_ref[:, lanes], gate_ref[:, lanes]).astype(BF))
        near_ref[:, lanes] = dot(inv_ref[...], spec_conj(spec, filt_of(long_ref, own)))


def fore_kernel(
    value_ref, k1_ref, q1_ref, k2_ref, q2_ref, k3_ref, rim_ref, filt_ref, rates_ref, back_ref,
    fwd_ref, inv_ref, med_ref,
    z1_ref, x1_ref, u2_ref, z2_ref, x2_ref, u3_ref, carry_ref, send_ref, ext, signal,
):
    count, width = value_ref.shape
    modes, groups = rates_ref.shape
    rim = rim_ref.shape[0] - 16
    for lanes, own in parts(width, groups):
        u1 = mul(k1_ref[:, lanes], value_ref[:, lanes]).astype(BF)
        ext[0:16, lanes] = rim_ref[rim : rim + 16, lanes].astype(F32)
        ext[16:, lanes] = u1.astype(F32)
        z1 = short_causal(ext, filt_ref, count, 16, lanes)
        z1_ref[:, lanes] = z1.astype(BF)
        x1 = mul(q1_ref[:, lanes], z1).astype(BF)
        x1_ref[:, lanes] = x1
        u2 = mul(k2_ref[:, lanes], x1).astype(BF)
        u2_ref[:, lanes] = u2
        spec = dot(fwd_ref[:, :count], u2)
        spec = spec + dot(fwd_ref[:, 2 * count - rim :], rim_ref[0:rim, lanes])
        z2 = dot(inv_ref[...], spec_mul(spec, filt_of(med_ref, own)))
        z2_ref[:, lanes] = z2.astype(BF)
        x2 = mul(q2_ref[:, lanes], z2).astype(BF)
        x2_ref[:, lanes] = x2
        u3 = mul(k3_ref[:, lanes], x2).astype(BF)
        u3_ref[:, lanes] = u3
        signal[:, lanes] = u3.astype(F32)
    carry_ref[0:modes, :] = back_ref[...]
    for lanes, own in parts(width, groups, LANES):
        carry_ref[modes:, lanes] = end_states(signal, rates_ref, lanes, own, False)
    send_ref[...] = carry_ref[...].astype(BF)


def back_long_kernel(
    flow, near_ref, state_ref, rates_ref, residues_ref, x2_ref, z2_ref, k3_ref, q2_ref, k2_ref, q1_ref,
    fwd_ref, inv_ref, med_ref,
    gk3_ref, gq2_ref, dz2_ref, du2_ref, rim_ref, far,
):
    count, width = near_ref.shape
    modes, groups = rates_ref.shape
    rim = rim_ref.shape[0] - 16
    for lanes, own in parts(width, groups, LANES):
        far_field(
            state_ref[0:modes, lanes], rates_ref[:, own], residues_ref[:, own], far, True, 1, lanes
        )
    for block, (lanes, own) in enumerate(parts(width, groups)):
        du3 = near_ref[:, lanes] + far[:, lanes]
        gk3_ref[:, lanes] = mul(du3, x2_ref[:, lanes]).astype(BF)
        dx2 = mul(du3, k3_ref[:, lanes]).astype(BF)
        gq2_ref[:, lanes] = mul(dx2, z2_ref[:, lanes]).astype(BF)
        dz2 = mul(dx2, q2_ref[:, lanes]).astype(BF)
        dz2_ref[:, lanes] = dz2
        spec = dot(fwd_ref[:, :count], dz2)
        du2 = dot(inv_ref[...], spec_conj(spec, filt_of(med_ref, own)))
        du2_ref[:, lanes] = du2
        rim_ref[0:rim, lanes] = dz2[0:rim]
        dx1 = mul(du2[0:16], k2_ref[0:16, lanes]).astype(BF)
        rim_ref[rim : rim + 16, lanes] = mul(dx1, q1_ref[0:16, lanes]).astype(BF)
        flow.flush(block)


def medium_terms_kernel(dz2_ref, u2_ref, rim_ref, fwd_ref, lag_ref, out_ref, total):
    count, width = dz2_ref.shape
    groups = out_ref.shape[1]
    rim = rim_ref.shape[0] - 16
    for lanes, own in parts(width, groups):
        ext = dot(fwd_ref[:, :count], u2_ref[:, lanes])
        ext = ext + dot(fwd_ref[:, 2 * count - rim :], rim_ref[0:rim, lanes])
        grad = dot(fwd_ref[:, :count], dz2_ref[:, lanes])
        er, ei, dr, di = ext[:count], ext[count:], grad[:count], grad[count:]
        edge = row_index(er.shape) == 0
        high = di * ei
        re = dr * er + jnp.where(edge, 0.0, high)
        im = jnp.where(edge, high, dr * ei - di * er)
        if lanes == own:
            total[:count, own] = re
            total[count:, own] = im
        else:
            total[:count, own] += re
            total[count:, own] += im
    out_ref[...] = dot(lag_ref[...], total[...].astype(BF))


def back_short_kernel(
    flow, du2_ref, rim_ref, x1_ref, z1_ref, k2_ref, q1_ref, k1_ref, value_ref, fore_ref, filt_ref,
    terms_ref, fwd_ref, inv_ref, med_ref,
    gk2_ref, gq1_ref, gk1_ref, gv_ref, send_ref, ext, signal, packet,
):
    count, width = du2_ref.shape
    groups = terms_ref.shape[1]
    rim = rim_ref.shape[0] - 16
    taps = filt_ref.shape[0]
    pieces = send_ref.shape[0]
    share = terms_ref.shape[0] // pieces
    half = groups // 2
    packet[...] = jnp.zeros_like(packet)
    for piece in range(pieces):
        rows = terms_ref[piece * share : (piece + 1) * share, :]
        packet[piece, 0:share, 0:half] = rows[:, :half]
        packet[piece, share : 2 * share, 0:half] = rows[:, half:]
    for block, (lanes, own) in enumerate(parts(width, groups)):
        spec = dot(fwd_ref[:, count : count + rim], rim_ref[0:rim, lanes])
        du2 = du2_ref[:, lanes] + dot(inv_ref[...], spec_conj(spec, filt_of(med_ref, own)))
        gk2_ref[:, lanes] = mul(du2, x1_ref[:, lanes]).astype(BF)
        dx1 = mul(du2, k2_ref[:, lanes]).astype(BF)
        gq1_ref[:, lanes] = mul(dx1, z1_ref[:, lanes]).astype(BF)
        dz1 = mul(dx1, q1_ref[:, lanes]).astype(BF).astype(F32)
        ext[0:count, lanes] = dz1
        ext[count:, lanes] = rim_ref[rim : rim + 16, lanes].astype(F32)
        signal[0:16, lanes] = fore_ref[rim : rim + 16, lanes].astype(F32)
        signal[16:, lanes] = mul(k1_ref[:, lanes], value_ref[:, lanes]).astype(BF).astype(F32)
        du1 = None
        for lag in range(taps):
            term = ext[pl.ds(lag, count), lanes] * filt_ref[lag : lag + 1, lanes].astype(F32)
            du1 = term if du1 is None else du1 + term
        gk1_ref[:, lanes] = mul(du1, value_ref[:, lanes]).astype(BF)
        gv_ref[:, lanes] = mul(du1, k1_ref[:, lanes]).astype(BF)
        flow.flush(block)
        for lag in range(taps):
            row = jnp.sum(dz1 * signal[pl.ds(16 - lag, count), lanes], axis=0, keepdims=True)
            spot = lag * (width // BLOCK) + block
            packet[spot, 0:1, half : half + LANES] = row[:, :LANES]
            packet[spot, 1:2, half : half + LANES] = row[:, LANES:]
    send_ref[...] = packet[...].astype(send_ref.dtype)


def fore_near_kernel(u3_ref, fwd_ref, inv_ref, long_ref, near_ref):
    count, width = u3_ref.shape
    for lanes, own in parts(width, long_ref.shape[2]):
        spec = dot(fwd_ref[:, :count], u3_ref[:, lanes])
        near_ref[:, lanes] = dot(inv_ref[...], spec_mul(spec, filt_of(long_ref, own)))


def fore_long_kernel(
    flow, near_ref, state_ref, rates_ref, residues_ref, q3_ref, grad_ref, mixed_ref, gq3_ref, far
):
    width = near_ref.shape[1]
    modes, groups = rates_ref.shape
    for block, (lanes, own) in enumerate(parts(width, groups)):
        for side in range(0, BLOCK, LANES):
            at = slice(lanes.start + side, lanes.start + side + LANES)
            mine = slice(own.start + side, own.start + side + LANES)
            far_field(
                state_ref[modes:, at], rates_ref[:, mine], residues_ref[:, mine], far, False, 1, at
            )
        z3 = far[:, lanes] + near_ref[:, lanes]
        mixed_ref[:, lanes] = mul(q3_ref[:, lanes], z3).astype(BF)
        gq3_ref[:, lanes] = mul(grad_ref[:, lanes], z3).astype(BF)
        flow.flush(block)


def scan_kernel(count, group, fan, size, refs):
    place_ref, rates_ref, total_ref = refs[:3]
    others = refs[3 : 2 + fan]
    rest = refs[2 + fan :]
    prefix_ref = None if group == 1 else rest[0]
    outs = rest if group == 1 else rest[1:]
    modes, groups = rates_ref.shape
    width = total_ref.shape[1]
    place = place_ref[0]
    last = group * fan >= size
    for side in range(2):
        rows = slice(side * modes, (side + 1) * modes)
        at = size - 1 - place if side == 0 else place
        mine = (at // group) % fan
        offset = at % group
        drop = rates_ref[...] * float(-count)

        def power(n, keep=None):
            value = jnp.exp(drop * n.astype(F32))
            return value if keep is None else jnp.where(keep, value, 0.0)

        for copy in range(width // groups):
            lanes = slice(copy * groups, (copy + 1) * groups)
            prefix = jnp.zeros((modes, groups), F32) if group == 1 else prefix_ref[rows, lanes]
            total = None
            if not last:
                total = total_ref[rows, lanes] * power(group * (fan - 1 - mine))
            for d, other in enumerate(others, 1):
                theirs = mine ^ d
                before = theirs < mine
                block = other[rows, lanes].astype(F32)
                gap = jnp.where(before, offset + group * (mine - 1 - theirs), 0)
                prefix = prefix + power(gap, before) * block
                if not last:
                    total = total + power(group * (fan - 1 - theirs)) * block
            outs[0][rows, lanes] = prefix
            if not last:
                outs[1][rows, lanes] = total
                outs[2][rows, lanes] = total.astype(BF)


def first_sum_kernel(got_ref, spread_ref, part_ref):
    part = jnp.sum(got_ref[...].astype(F32), axis=0)
    part_ref[...] = part
    half = spread_ref.shape[2]
    spread_ref[...] = jnp.broadcast_to(part[None, :, :half], spread_ref.shape).astype(
        spread_ref.dtype
    )


def second_sum_kernel(got_ref, part_ref, piece_ref):
    medium = jnp.sum(got_ref[...].astype(F32), axis=0)
    half = medium.shape[1]
    piece = jnp.concatenate([medium, part_ref[:, half:]], axis=1)
    piece_ref[...] = jnp.broadcast_to(piece[None], piece_ref.shape).astype(piece_ref.dtype)


def collect_kernel(full_ref, short_ref, medium_ref):
    pieces = full_ref.shape[0]
    half = medium_ref.shape[1] // 2
    share = medium_ref.shape[0] // pieces
    for piece in range(pieces):
        rows = full_ref[piece].astype(F32)
        place = slice(piece * share, (piece + 1) * share)
        medium_ref[place, :half] = rows[0:share, :half]
        medium_ref[place, half:] = rows[share : 2 * share, :half]
    blocks = short_ref.shape[1] // BLOCK
    for lag in range(short_ref.shape[0]):
        for block in range(blocks):
            rows = full_ref[lag * blocks + block].astype(F32)
            for side in range(2):
                start = block * BLOCK + side * LANES
                short_ref[lag : lag + 1, start : start + LANES] = rows[side : side + 1, half:]


def swapped(block, distance):
    size = lax.axis_size("ctx")
    return lax.ppermute(block, "ctx", [(i, i ^ distance) for i in range(size)])


def shifted(block, distance):
    size = lax.axis_size("ctx")
    route = [(i, i + distance) for i in range(size) if 0 <= i + distance < size]
    return lax.ppermute(block, "ctx", route)


def exchanged(block, axis):
    return lax.all_to_all(block, axis, 0, 0)


def axes():
    return lax.axis_size("ctx"), lax.axis_size("tp"), lax.axis_index("ctx")


def shape(rows, cols, dtype=BF):
    return jax.ShapeDtypeStruct((rows, cols), dtype)


class Big:
    def __init__(self, array, block=BLOCK, kept=False):
        self.array, self.block, self.kept = array, block, kept

    def lanes(self):
        width = self.array.shape[-1]
        return [slice(k, k + self.block) for k in range(0, width, self.block)]


class Held:
    def __init__(self, array):
        self.array = array


class Moves:
    def __init__(self, sources, targets, arrays, sems):
        self.copies, count = {}, 0
        for piece in range(max([len(a.lanes()) for a in arrays], default=0)):
            for source, target, array in zip(sources, targets, arrays):
                if piece < len(array.lanes()):
                    at = (slice(None),) * (len(array.array.shape) - 1) + (array.lanes()[piece],)
                    copy = pltpu.make_async_copy(source.at[at], target.at[at], sems.at[count])
                    self.copies.setdefault(piece, []).append(copy)
                    count += 1

    def start(self, piece):
        for copy in self.copies.get(piece, []):
            copy.start()

    def wait(self, piece):
        for copy in self.copies.get(piece, []):
            copy.wait()


class Flow:
    def __init__(self, loads, stores):
        self.loads, self.stores = loads, stores
        for piece in loads.copies:
            loads.start(piece)

    def ready(self, piece):
        self.loads.wait(piece)

    def flush(self, piece):
        self.stores.start(piece)


def call(kernel, name, out_shape, *scratch, scalars=0):
    outs = out_shape if isinstance(out_shape, list) else [out_shape]

    def typed(o):
        if isinstance(o, Big):
            return pltpu.HBM(o.array.shape, o.array.dtype)
        return pltpu.VMEM(o.array.shape, o.array.dtype) if isinstance(o, Held) else o

    def placed(a):
        if isinstance(a, Big):
            return pltpu.with_memory_space_constraint(a.array, pltpu.HBM)
        if isinstance(a, Held):
            return pltpu.with_memory_space_constraint(a.array, pltpu.VMEM)
        return a

    def run(*args):
        big_in = [a for a in args if isinstance(a, Big)]
        kept = [a for a in big_in if a.kept]
        big_out = [o for o in outs if isinstance(o, Big)]

        def body(*refs):
            ins, rest = list(refs[: len(args)]), refs[len(args) :]
            results, rest = list(rest[: len(outs)]), rest[len(outs) :]
            held_kept, rest = iter(rest[: len(kept)]), rest[len(kept) :]
            fresh = len(big_in) - len(kept)
            held_new, rest = iter(rest[:fresh]), rest[fresh:]
            held_in = [next(held_kept) if a.kept else next(held_new) for a in big_in]
            held_out, rest = rest[: len(big_out)], rest[len(big_out) :]
            own, sems = rest[: len(scratch)], rest[len(scratch) :]
            if not big_in and not big_out:
                kernel(*ins, *results, *own)
                return
            at_in = [k for k, a in enumerate(args) if isinstance(a, Big)]
            at_out = [k for k, o in enumerate(outs) if isinstance(o, Big)]
            loads = Moves([ins[k] for k in at_in], held_in, big_in, sems[0])
            stores = Moves(held_out, [results[k] for k in at_out], big_out, sems[1])
            for k, ref in zip(at_in, held_in):
                ins[k] = ref
            for k, ref in zip(at_out, held_out):
                results[k] = ref
            kernel(Flow(loads, stores), *ins, *results, *own)
            for piece in stores.copies:
                stores.wait(piece)

        def place(a, k=None):
            if isinstance(a, Big):
                return pl.BlockSpec(memory_space=pltpu.HBM)
            return pl.BlockSpec(memory_space=pltpu.SMEM if k is not None and k < scalars else pltpu.VMEM)

        held = [pltpu.VMEM(a.array.shape, a.array.dtype) for a in big_in + big_out if not a.kept]
        sems = []
        if big_in or big_out:
            for group in (big_in, big_out):
                sems.append(pltpu.SemaphoreType.DMA((max(1, sum(len(a.lanes()) for a in group)),)))
        got = pl.pallas_call(
            body,
            name=name,
            in_specs=[place(a, k) for k, a in enumerate(args)],
            out_specs=[place(o) for o in outs] + [place(None)] * len(kept),
            out_shape=[typed(o) for o in outs] + [typed(Held(a.array)) for a in kept],
            scratch_shapes=held + [pltpu.VMEM(c, F32) for c in scratch] + sems,
            compiler_params=pltpu.CompilerParams(vmem_limit_bytes=VMEM_LIMIT),
        )(*[placed(a) for a in args])
        return got if isinstance(out_shape, list) or kept else got[0]

    return run


def after(array, other):
    return lax.optimization_barrier((array, other))[0]


def scan_states(total, send, rates, count, place, size, works):
    modes2, width = total.shape
    prefix = ()
    group = 1
    done = []
    for fan, work in zip((2, 4, 4), works):
        others = [swapped(send, d * group) for d in range(1, fan)]
        done.append(work(send, *done))
        total = after(total, done[-1])
        last = group * fan >= size
        outs = [shape(modes2, width, F32)]
        if not last:
            outs += [shape(modes2, width, F32), shape(modes2, width)]

        def kernel(*refs, group=group, fan=fan):
            scan_kernel(count, group, fan, size, refs)

        got = call(kernel, "scan%d" % group, outs, scalars=1)(place, rates, total, *others, *prefix)
        prefix = (got[0],)
        if not last:
            total, send = got[1], got[2]
        group *= fan
    return prefix[0], done


def on_device(
    value, gate_q1, gate_k1, gate_q2, gate_k2, gate_q3, gate_k3, grad_out,
    short_filter, medium_filter, residues, rates,
):
    count, width = value.shape
    modes, groups = rates.shape
    taps, rim = short_filter.shape[0], medium_filter.shape[0]
    ctx, tp, place = axes()
    place = jnp.reshape(place, (1,)).astype(jnp.int32)
    forward, backward = dft_tables(count)
    fwd32 = jnp.asarray(forward[:, :count], F32)
    fwd = jnp.asarray(forward, BF)
    inv = jnp.asarray(backward[:count], BF)
    lag = jnp.asarray(backward[(-np.arange(rim)) % (2 * count)], BF)
    value, gate_q1, gate_k1, gate_q2, gate_k2, gate_q3, gate_k3, grad_out = [
        Big(a, kept=True)
        for a in (value, gate_q1, gate_k1, gate_q2, gate_k2, gate_q3, gate_k3, grad_out)
    ]
    tables = [Big(t, t.shape[1], kept=True) for t in (fwd32, fwd, inv, lag)]
    full, ext_full = Big(shape(count, width)), (count + 16, width)
    kept, wide = Held(shape(count, width)), Held(shape(count, width, F32))
    filters = Held(jax.ShapeDtypeStruct((3, count, groups), F32))

    def hold(arrays):
        return [Held(a) for a in arrays]

    rim_send, *got = call(
        fore_rim_kernel, "fore_rim", shape(rim + 16, width), (rim + 16, width), scalars=1
    )(place, value, gate_k1, gate_q1, gate_k2, short_filter)
    value, gate_k1, gate_q1, gate_k2 = hold(got)
    rim_fore = shifted(rim_send, 1)
    got = call(medium_filter_kernel, "medium_filter", filters)(
        tables[0], medium_filter, *tables[1:], grad_out, gate_q3, gate_q2, gate_k3
    )
    med, fwd32, fwd, inv, lag, grad_out, gate_q3, gate_q2, gate_k3 = hold(got)
    back_carry = call(back_carry_kernel, "back_carry", shape(modes, width, F32), (count, width))(
        grad_out, gate_q3, rates
    )

    got = call(
        fore_kernel, "fore",
        [kept] * 6 + [shape(2 * modes, width, F32), shape(2 * modes, width)],
        ext_full, (count, width),
    )(value, gate_k1, gate_q1, gate_k2, gate_q2, gate_k3, rim_fore, short_filter, rates, back_carry,
      fwd, inv, med)
    z1, x1, u2, z2, x2, u3 = hold(got[:6])
    carry, send = got[6:]

    def long_filter(start):
        return call(long_filter_kernel, "long_filter", filters, (count, groups))(
            fwd32, residues, after(rates, start)
        )

    def back_near(start, lng):
        return call(back_near_kernel, "back_near", wide)(
            grad_out, gate_q3, fwd, inv, Held(after(lng, start))
        )

    def fore_near(start, lng, _):
        return call(fore_near_kernel, "fore_near", wide)(u3, fwd, inv, Held(after(lng, start)))

    states, (_, du3_near, z3_near) = scan_states(
        carry, send, rates, count, place, ctx, (long_filter, back_near, fore_near)
    )

    grad_k3, grad_q2, dz2, du2_near, rim_back_send = call(
        back_long_kernel, "back_long", [full] * 2 + [kept, wide, shape(rim + 16, width)], (count, width)
    )(Held(du3_near), states, rates, residues, x2, z2, gate_k3, gate_q2, gate_k2, gate_q1, fwd, inv, med)
    dz2, du2_near = Held(dz2), Held(du2_near)
    rim_back = shifted(rim_back_send, -1)

    terms = call(medium_terms_kernel, "medium_terms", shape(rim, groups, F32), (2 * count, groups))(
        dz2, u2, rim_fore, fwd, lag
    )
    mixed, grad_q3 = call(fore_long_kernel, "fore_long", [full] * 2, (count, width))(
        Held(z3_near), states, rates, residues, gate_q3, grad_out
    )
    terms = after(terms, mixed)

    packet = (ctx, 8, groups // 2 + LANES)
    grad_k2, grad_q1, grad_k1, grad_value, out = call(
        back_short_kernel, "back_short",
        [full] * 4 + [jax.ShapeDtypeStruct(packet, BF)], ext_full, ext_full, packet,
    )(du2_near, rim_back, x1, z1, gate_k2, gate_q1, gate_k1, value, rim_fore, short_filter, terms,
      fwd, inv, med)

    spread, part = call(
        first_sum_kernel, "first_sum",
        [jax.ShapeDtypeStruct((tp, 8, groups // 2), BF), shape(8, packet[2], F32)],
    )(exchanged(out, "ctx"))
    piece = call(second_sum_kernel, "second_sum", jax.ShapeDtypeStruct(packet, BF))(
        exchanged(spread, "tp"), part
    )
    grad_short, grad_medium = call(
        collect_kernel, "collect", [shape(taps, width, F32), shape(rim, groups, F32)]
    )(exchanged(piece, "ctx"))
    return (
        mixed, grad_value, grad_q1, grad_k1, grad_q2, grad_k2, grad_q3, grad_k3, grad_short, grad_medium,
    )


def solution(mesh):
    data = P("ctx", "tp")
    return jax.shard_map(
        on_device,
        mesh=mesh,
        in_specs=(data,) * 8 + (P(None, "tp"), P(), P(), P()),
        out_specs=(data,) * 8 + (P(None, "tp"), P()),
        check_vma=False,
    )
```

```python
import jax
import jax.numpy as jnp
import numpy as np
from jax import lax
from jax.experimental import pallas as pl
from jax.experimental.pallas import tpu as pltpu
from jax.sharding import PartitionSpec as P

F32 = jnp.float32
BF = jnp.bfloat16
LANES = 128
VMEM_LIMIT = 28 * 1024 * 1024
BLOCK = 256
WIDE = 512
UNROLL = 16
LATE = 99


def dft_tables(count):
    size = 2 * count
    freq = np.arange(count)[:, None].astype(np.int64)

    def waves(times):
        phase = (freq * times[None, :]) % size * (2.0 * np.pi / size)
        cosine, sine = np.cos(phase), -np.sin(phase)
        sine[0] = np.where(times % 2 == 0, 1.0, -1.0)
        return np.concatenate([cosine, sine], axis=0)

    forward = waves(np.arange(size))
    scale = np.full((size, 1), 2.0 / size)
    scale[0] = scale[count] = 1.0 / size
    backward = (forward * scale).T
    return forward, backward


def dot(a, b):
    return jnp.dot(a, b, preferred_element_type=F32)


def spec_mul(spec, filt):
    half = spec.shape[0] // 2
    re, im = spec[:half], spec[half:]
    a, b, c = filt
    return jnp.concatenate([(re * a - im * b).astype(BF), (re * b + im * c).astype(BF)], axis=0)


def spec_conj(spec, filt):
    half = spec.shape[0] // 2
    re, im = spec[:half], spec[half:]
    a, b, c = filt
    return jnp.concatenate([(re * a + im * b).astype(BF), (im * c - re * b).astype(BF)], axis=0)


def row_index(shape):
    return lax.broadcasted_iota(jnp.int32, shape, 0)


def end_states(signal_ref, rates_ref, lanes, own, reverse):
    tiles = signal_ref.shape[0] // 8
    modes = rates_ref.shape[0]
    rates = rates_ref[:, own]
    step = jnp.exp(-8.0 * rates)
    steps = [jnp.broadcast_to(step[m : m + 1], (8, LANES)) for m in range(modes)]

    def body(j, sums):
        tile = tiles - 1 - j if reverse else j
        u = signal_ref[pl.ds(pl.multiple_of(tile * 8, 8), 8), lanes]
        return tuple(s * a + u for s, a in zip(sums, steps))

    zero = jnp.zeros((8, LANES), F32)
    sums = lax.fori_loop(0, tiles, body, (zero,) * modes, unroll=UNROLL)
    sub = row_index((8, LANES)).astype(F32)
    ages = sub if reverse else 7.0 - sub
    rows = [
        jnp.sum(s * jnp.exp(-rates[m : m + 1] * ages), axis=0, keepdims=True)
        for m, s in enumerate(sums)
    ]
    return jnp.concatenate(rows, axis=0)


def far_field(states, rates, weights, out_ref, reverse, first, lanes):
    tiles = out_ref.shape[0] // 8
    modes = rates.shape[0]
    weights = weights * jnp.sqrt(2.0 * rates)
    if states is not None:
        weights = weights * states
    step = jnp.exp(-8.0 * rates)
    steps = [jnp.broadcast_to(step[m : m + 1], (8, LANES)) for m in range(modes)]
    sub = row_index((8, LANES)).astype(F32)
    ages = (7.0 - sub if reverse else sub) + float(first)
    terms = tuple(weights[m : m + 1] * jnp.exp(-rates[m : m + 1] * ages) for m in range(modes))

    def body(j, terms):
        tile = tiles - 1 - j if reverse else j
        level = list(terms)
        while len(level) > 1:
            level = [level[i] + level[i + 1] for i in range(0, len(level), 2)]
        out_ref[pl.ds(pl.multiple_of(tile * 8, 8), 8), lanes] = level[0]
        return tuple(s * a for s, a in zip(terms, steps))

    lax.fori_loop(0, tiles, body, terms, unroll=UNROLL)


def parts(width, groups, size=BLOCK):
    for start in range(0, width, size):
        own = start % groups
        yield slice(start, start + size), slice(own, own + size)


def mul(a, b):
    return a.astype(F32) * b.astype(F32)


def short_causal(ext, filt, rows, start, lanes):
    total = None
    for lag in range(filt.shape[0]):
        term = ext[pl.ds(start - lag, rows), lanes] * filt[lag : lag + 1, lanes].astype(F32)
        total = term if total is None else total + term
    return total


def fore_rim_kernel(
    flow, place_ref, filt_ref, value_ref, k1_ref, q1_ref, k2_ref, out_ref, *refs
):
    ext = refs[-1]
    del place_ref
    count, width = value_ref.shape
    rim = out_ref.shape[0] - 16
    top = count - rim - 16
    for block, (lanes, _) in enumerate(parts(width, width)):
        flow.ready(block)
        u1 = mul(k1_ref[top:, lanes], value_ref[top:, lanes]).astype(BF)
        ext[:, lanes] = u1.astype(F32)
        z1 = short_causal(ext, filt_ref, rim, 16, lanes)
        x1 = mul(q1_ref[count - rim :, lanes], z1).astype(BF)
        out_ref[0:rim, lanes] = mul(k2_ref[count - rim :, lanes], x1).astype(BF)
        out_ref[rim : rim + 16, lanes] = u1[rim:]


def spectrum(table, filt, out):
    count = out.shape[1]
    spec = jnp.dot(
        table[:, : filt.shape[0]], filt, precision=lax.Precision.HIGHEST, preferred_element_type=F32
    )
    re, im = spec[:count], spec[count:]
    edge = row_index(re.shape) == 0
    out[0] = re
    out[1] = jnp.where(edge, 0.0, im)
    out[2] = jnp.where(edge, im, re)


def medium_filter_kernel(flow, table_ref, medium_ref, *refs):
    out_ref = refs[-1]
    flow.ready(0)
    spectrum(table_ref, medium_ref[...].astype(F32), out_ref)
    for piece in range(1, 4):
        flow.ready(piece)


def long_filter_kernel(table_ref, residues_ref, rates_ref, out_ref, local):
    for lanes, _ in parts(local.shape[1], local.shape[1], LANES):
        far_field(None, rates_ref[:, lanes], residues_ref[:, lanes], local, False, 0, lanes)
    spectrum(table_ref, local[...], out_ref)


def filt_of(ref, own):
    return ref[0, :, own], ref[1, :, own], ref[2, :, own]


def back_carry_kernel(grad_ref, gate_ref, rates_ref, carry_ref, signal):
    count, width = grad_ref.shape
    groups = rates_ref.shape[1]
    for lanes, own in parts(width, groups):
        signal[:, lanes] = mul(grad_ref[:, lanes], gate_ref[:, lanes])
        for side in range(0, BLOCK, LANES):
            at = slice(lanes.start + side, lanes.start + side + LANES)
            mine = slice(own.start + side, own.start + side + LANES)
            carry_ref[:, at] = end_states(signal, rates_ref, at, mine, True)


def back_near_kernel(grad_ref, gate_ref, fwd_ref, inv_ref, long_ref, near_ref):
    count, width = grad_ref.shape
    for lanes, own in parts(width, long_ref.shape[2]):
        spec = dot(fwd_ref[:, :count], mul(grad_ref[:, lanes], gate_ref[:, lanes]).astype(BF))
        near_ref[:, lanes] = dot(inv_ref[...], spec_conj(spec, filt_of(long_ref, own)))


def fore_kernel(
    value_ref, k1_ref, q1_ref, k2_ref, q2_ref, k3_ref, rim_ref, filt_ref, rates_ref, back_ref,
    fwd_ref, inv_ref, med_ref,
    z1_ref, x1_ref, u2_ref, z2_ref, x2_ref, u3_ref, carry_ref, send_ref, ext, signal,
):
    count, width = value_ref.shape
    modes, groups = rates_ref.shape
    rim = rim_ref.shape[0] - 16
    for lanes, own in parts(width, groups, WIDE):
        u1 = mul(k1_ref[:, lanes], value_ref[:, lanes]).astype(BF)
        ext[0:16, lanes] = rim_ref[rim : rim + 16, lanes].astype(F32)
        ext[16:, lanes] = u1.astype(F32)
        z1 = short_causal(ext, filt_ref, count, 16, lanes)
        z1_ref[:, lanes] = z1.astype(BF)
        x1 = mul(q1_ref[:, lanes], z1).astype(BF)
        x1_ref[:, lanes] = x1
        u2 = mul(k2_ref[:, lanes], x1).astype(BF)
        u2_ref[:, lanes] = u2
        spec = dot(fwd_ref[:, :count], u2)
        spec = spec + dot(fwd_ref[:, 2 * count - rim :], rim_ref[0:rim, lanes])
        z2 = dot(inv_ref[...], spec_mul(spec, filt_of(med_ref, own)))
        z2_ref[:, lanes] = z2.astype(BF)
        x2 = mul(q2_ref[:, lanes], z2).astype(BF)
        x2_ref[:, lanes] = x2
        u3 = mul(k3_ref[:, lanes], x2).astype(BF)
        u3_ref[:, lanes] = u3
        signal[:, lanes] = u3.astype(F32)
    carry_ref[0:modes, :] = back_ref[...]
    for lanes, own in parts(width, groups, LANES):
        carry_ref[modes:, lanes] = end_states(signal, rates_ref, lanes, own, False)
    send_ref[...] = carry_ref[...].astype(BF)


def back_long_kernel(
    near_ref, state_ref, rates_ref, residues_ref, k3_ref, q2_ref, k2_ref, q1_ref,
    fwd_ref, inv_ref, med_ref,
    du3_ref, dz2_ref, spec_ref, rim_ref, far,
):
    count, width = near_ref.shape
    modes, groups = rates_ref.shape
    rim = rim_ref.shape[0] - 16
    for lanes, own in parts(width, groups, LANES):
        far_field(
            state_ref[0:modes, lanes], rates_ref[:, own], residues_ref[:, own], far, True, 1, lanes
        )
    for lanes, own in parts(width, groups, WIDE):
        du3 = near_ref[:, lanes] + far[:, lanes]
        du3_ref[:, lanes] = du3
        dx2 = mul(du3, k3_ref[:, lanes]).astype(BF)
        dz2 = mul(dx2, q2_ref[:, lanes]).astype(BF)
        dz2_ref[:, lanes] = dz2
        spec = spec_conj(dot(fwd_ref[:, :count], dz2), filt_of(med_ref, own))
        spec_ref[:, lanes] = spec
        rim_ref[0:rim, lanes] = dz2[0:rim]
        dx1 = mul(dot(inv_ref[0:16, :], spec), k2_ref[0:16, lanes]).astype(BF)
        rim_ref[rim : rim + 16, lanes] = mul(dx1, q1_ref[0:16, lanes]).astype(BF)


def back_rest_kernel(
    flow, du3_ref, spec_ref, x2_ref, z2_ref, k3_ref, inv_ref, gk3_ref, gq2_ref, du2_ref
):
    width = du3_ref.shape[1]
    for block, (lanes, _) in enumerate(parts(width, width)):
        du2_ref[:, lanes] = dot(inv_ref[...], spec_ref[:, lanes])
        du3 = du3_ref[:, lanes]
        gk3_ref[:, lanes] = mul(du3, x2_ref[:, lanes]).astype(BF)
        dx2 = mul(du3, k3_ref[:, lanes]).astype(BF)
        gq2_ref[:, lanes] = mul(dx2, z2_ref[:, lanes]).astype(BF)
        flow.flush(block)


def medium_terms_kernel(dz2_ref, u2_ref, rim_ref, fwd_ref, lag_ref, out_ref, total):
    count, width = dz2_ref.shape
    groups = out_ref.shape[1]
    rim = rim_ref.shape[0] - 16
    for lanes, own in parts(width, groups):
        ext = dot(fwd_ref[:, :count], u2_ref[:, lanes])
        ext = ext + dot(fwd_ref[:, 2 * count - rim :], rim_ref[0:rim, lanes])
        grad = dot(fwd_ref[:, :count], dz2_ref[:, lanes])
        er, ei, dr, di = ext[:count], ext[count:], grad[:count], grad[count:]
        edge = row_index(er.shape) == 0
        high = di * ei
        re = dr * er + jnp.where(edge, 0.0, high)
        im = jnp.where(edge, high, dr * ei - di * er)
        if lanes == own:
            total[:count, own] = re
            total[count:, own] = im
        else:
            total[:count, own] += re
            total[count:, own] += im
    out_ref[...] = dot(lag_ref[...], total[...].astype(BF))


def back_short_kernel(
    flow, du2_ref, rim_ref, x1_ref, z1_ref, k2_ref, q1_ref, k1_ref, value_ref, fore_ref, filt_ref,
    terms_ref, fwd_ref, inv_ref, med_ref,
    gk2_ref, gq1_ref, gk1_ref, gv_ref, send_ref, ext, signal, packet,
):
    count, width = du2_ref.shape
    groups = terms_ref.shape[1]
    rim = rim_ref.shape[0] - 16
    taps = filt_ref.shape[0]
    pieces = send_ref.shape[0]
    share = terms_ref.shape[0] // pieces
    half = groups // 2
    packet[...] = jnp.zeros_like(packet)
    for piece in range(pieces):
        rows = terms_ref[piece * share : (piece + 1) * share, :]
        packet[piece, 0:share, 0:half] = rows[:, :half]
        packet[piece, share : 2 * share, 0:half] = rows[:, half:]
    for block, (lanes, own) in enumerate(parts(width, groups)):
        spec = dot(fwd_ref[:, count : count + rim], rim_ref[0:rim, lanes])
        du2 = du2_ref[:, lanes] + dot(inv_ref[...], spec_conj(spec, filt_of(med_ref, own)))
        gk2_ref[:, lanes] = mul(du2, x1_ref[:, lanes]).astype(BF)
        dx1 = mul(du2, k2_ref[:, lanes]).astype(BF)
        gq1_ref[:, lanes] = mul(dx1, z1_ref[:, lanes]).astype(BF)
        dz1 = mul(dx1, q1_ref[:, lanes]).astype(BF).astype(F32)
        ext[0:count, lanes] = dz1
        ext[count:, lanes] = rim_ref[rim : rim + 16, lanes].astype(F32)
        signal[0:16, lanes] = fore_ref[rim : rim + 16, lanes].astype(F32)
        signal[16:, lanes] = mul(k1_ref[:, lanes], value_ref[:, lanes]).astype(BF).astype(F32)
        du1 = None
        for lag in range(taps):
            term = ext[pl.ds(lag, count), lanes] * filt_ref[lag : lag + 1, lanes].astype(F32)
            du1 = term if du1 is None else du1 + term
        gk1_ref[:, lanes] = mul(du1, value_ref[:, lanes]).astype(BF)
        gv_ref[:, lanes] = mul(du1, k1_ref[:, lanes]).astype(BF)
        flow.flush(block)
        for lag in range(taps):
            row = jnp.sum(dz1 * signal[pl.ds(16 - lag, count), lanes], axis=0, keepdims=True)
            spot = lag * (width // BLOCK) + block
            packet[spot, 0:1, half : half + LANES] = row[:, :LANES]
            packet[spot, 1:2, half : half + LANES] = row[:, LANES:]
    send_ref[...] = packet[...].astype(send_ref.dtype)


def fore_near_kernel(u3_ref, fwd_ref, inv_ref, long_ref, near_ref):
    count, width = u3_ref.shape
    for lanes, own in parts(width, long_ref.shape[2]):
        spec = dot(fwd_ref[:, :count], u3_ref[:, lanes])
        near_ref[:, lanes] = dot(inv_ref[...], spec_mul(spec, filt_of(long_ref, own)))


def fore_long_kernel(
    flow, near_ref, state_ref, rates_ref, residues_ref, q3_ref, grad_ref, mixed_ref, gq3_ref, far
):
    width = near_ref.shape[1]
    modes, groups = rates_ref.shape
    for block, (lanes, own) in enumerate(parts(width, groups)):
        for side in range(0, BLOCK, LANES):
            at = slice(lanes.start + side, lanes.start + side + LANES)
            mine = slice(own.start + side, own.start + side + LANES)
            far_field(
                state_ref[modes:, at], rates_ref[:, mine], residues_ref[:, mine], far, False, 1, at
            )
        z3 = far[:, lanes] + near_ref[:, lanes]
        mixed_ref[:, lanes] = mul(q3_ref[:, lanes], z3).astype(BF)
        gq3_ref[:, lanes] = mul(grad_ref[:, lanes], z3).astype(BF)
        flow.flush(block)


def scan_kernel(count, group, fan, size, refs):
    place_ref, rates_ref, total_ref = refs[:3]
    others = refs[3 : 2 + fan]
    rest = refs[2 + fan :]
    prefix_ref = None if group == 1 else rest[0]
    outs = rest if group == 1 else rest[1:]
    modes, groups = rates_ref.shape
    width = total_ref.shape[1]
    place = place_ref[0]
    last = group * fan >= size
    for side in range(2):
        rows = slice(side * modes, (side + 1) * modes)
        at = size - 1 - place if side == 0 else place
        mine = (at // group) % fan
        offset = at % group
        drop = rates_ref[...] * float(-count)

        def power(n, keep=None):
            value = jnp.exp(drop * n.astype(F32))
            return value if keep is None else jnp.where(keep, value, 0.0)

        for copy in range(width // groups):
            lanes = slice(copy * groups, (copy + 1) * groups)
            prefix = jnp.zeros((modes, groups), F32) if group == 1 else prefix_ref[rows, lanes]
            total = None
            if not last:
                total = total_ref[rows, lanes] * power(group * (fan - 1 - mine))
            for d, other in enumerate(others, 1):
                theirs = mine ^ d
                before = theirs < mine
                block = other[rows, lanes].astype(F32)
                gap = jnp.where(before, offset + group * (mine - 1 - theirs), 0)
                prefix = prefix + power(gap, before) * block
                if not last:
                    total = total + power(group * (fan - 1 - theirs)) * block
            outs[0][rows, lanes] = prefix
            if not last:
                outs[1][rows, lanes] = total
                outs[2][rows, lanes] = total.astype(BF)


def first_sum_kernel(got_ref, spread_ref, part_ref):
    part = jnp.sum(got_ref[...].astype(F32), axis=0)
    part_ref[...] = part
    half = spread_ref.shape[2]
    spread_ref[...] = jnp.broadcast_to(part[None, :, :half], spread_ref.shape).astype(
        spread_ref.dtype
    )


def second_sum_kernel(got_ref, part_ref, piece_ref):
    medium = jnp.sum(got_ref[...].astype(F32), axis=0)
    half = medium.shape[1]
    piece = jnp.concatenate([medium, part_ref[:, half:]], axis=1)
    piece_ref[...] = jnp.broadcast_to(piece[None], piece_ref.shape).astype(piece_ref.dtype)


def collect_kernel(full_ref, short_ref, medium_ref):
    pieces = full_ref.shape[0]
    half = medium_ref.shape[1] // 2
    share = medium_ref.shape[0] // pieces
    for piece in range(pieces):
        rows = full_ref[piece].astype(F32)
        place = slice(piece * share, (piece + 1) * share)
        medium_ref[place, :half] = rows[0:share, :half]
        medium_ref[place, half:] = rows[share : 2 * share, :half]
    blocks = short_ref.shape[1] // BLOCK
    for lag in range(short_ref.shape[0]):
        for block in range(blocks):
            rows = full_ref[lag * blocks + block].astype(F32)
            for side in range(2):
                start = block * BLOCK + side * LANES
                short_ref[lag : lag + 1, start : start + LANES] = rows[side : side + 1, half:]


def swapped(block, distance):
    size = lax.axis_size("ctx")
    return lax.ppermute(block, "ctx", [(i, i ^ distance) for i in range(size)])


def shifted(block, distance):
    size = lax.axis_size("ctx")
    route = [(i, i + distance) for i in range(size) if 0 <= i + distance < size]
    return lax.ppermute(block, "ctx", route)


def exchanged(block, axis):
    return lax.all_to_all(block, axis, 0, 0)


def axes():
    return lax.axis_size("ctx"), lax.axis_size("tp"), lax.axis_index("ctx")


def shape(rows, cols, dtype=BF):
    return jax.ShapeDtypeStruct((rows, cols), dtype)


class Big:
    def __init__(self, array, block=BLOCK, kept=False, head=0):
        self.array, self.block, self.kept, self.head = array, block, kept, head

    def count(self):
        return len(self.lanes()) * (2 if self.head else 1)

    def boxes(self, piece):
        lead = (slice(None),) * (len(self.array.shape) - 1)
        lanes = (self.lanes()[piece],)
        if not self.head:
            return [(piece, lead + lanes)]
        top = (slice(0, self.head),) + lanes
        return [(piece, (slice(self.head, self.array.shape[0]),) + lanes), (LATE, top)]

    def lanes(self):
        width = self.array.shape[-1]
        return [slice(k, k + self.block) for k in range(0, width, self.block)]


class Held:
    def __init__(self, array):
        self.array = array


class Moves:
    def __init__(self, sources, targets, arrays, sems):
        self.copies, count = {}, 0
        for piece in range(max([len(a.lanes()) for a in arrays], default=0)):
            for source, target, array in zip(sources, targets, arrays):
                if piece < len(array.lanes()):
                    for key, at in array.boxes(piece):
                        copy = pltpu.make_async_copy(source.at[at], target.at[at], sems.at[count])
                        self.copies.setdefault(key, []).append(copy)
                        count += 1

    def start(self, piece):
        for copy in self.copies.get(piece, []):
            copy.start()

    def wait(self, piece):
        for copy in self.copies.get(piece, []):
            copy.wait()


class Flow:
    def __init__(self, loads, stores):
        self.loads, self.stores = loads, stores
        for piece in sorted(loads.copies):
            loads.start(piece)

    def ready(self, piece):
        self.loads.wait(piece)

    def flush(self, piece):
        self.stores.start(piece)


def call(kernel, name, out_shape, *scratch, scalars=0):
    outs = out_shape if isinstance(out_shape, list) else [out_shape]

    def typed(o):
        if isinstance(o, Big):
            return pltpu.HBM(o.array.shape, o.array.dtype)
        return pltpu.VMEM(o.array.shape, o.array.dtype) if isinstance(o, Held) else o

    def placed(a):
        if isinstance(a, Big):
            return pltpu.with_memory_space_constraint(a.array, pltpu.HBM)
        if isinstance(a, Held):
            return pltpu.with_memory_space_constraint(a.array, pltpu.VMEM)
        return a

    def run(*args):
        big_in = [a for a in args if isinstance(a, Big)]
        kept = [a for a in big_in if a.kept]
        big_out = [o for o in outs if isinstance(o, Big)]

        def body(*refs):
            ins, rest = list(refs[: len(args)]), refs[len(args) :]
            results, rest = list(rest[: len(outs)]), rest[len(outs) :]
            held_kept, rest = iter(rest[: len(kept)]), rest[len(kept) :]
            fresh = len(big_in) - len(kept)
            held_new, rest = iter(rest[:fresh]), rest[fresh:]
            held_in = [next(held_kept) if a.kept else next(held_new) for a in big_in]
            held_out, rest = rest[: len(big_out)], rest[len(big_out) :]
            own, sems = rest[: len(scratch)], rest[len(scratch) :]
            if not big_in and not big_out:
                kernel(*ins, *results, *own)
                return
            at_in = [k for k, a in enumerate(args) if isinstance(a, Big)]
            at_out = [k for k, o in enumerate(outs) if isinstance(o, Big)]
            loads = Moves([ins[k] for k in at_in], held_in, big_in, sems[0])
            stores = Moves(held_out, [results[k] for k in at_out], big_out, sems[1])
            for k, ref in zip(at_in, held_in):
                ins[k] = ref
            for k, ref in zip(at_out, held_out):
                results[k] = ref
            kernel(Flow(loads, stores), *ins, *results, *own)
            loads.wait(LATE)
            for piece in stores.copies:
                stores.wait(piece)

        def place(a, k=None):
            if isinstance(a, Big):
                return pl.BlockSpec(memory_space=pltpu.HBM)
            return pl.BlockSpec(memory_space=pltpu.SMEM if k is not None and k < scalars else pltpu.VMEM)

        held = [pltpu.VMEM(a.array.shape, a.array.dtype) for a in big_in + big_out if not a.kept]
        sems = []
        if big_in or big_out:
            for group in (big_in, big_out):
                sems.append(pltpu.SemaphoreType.DMA((max(1, sum(a.count() for a in group)),)))
        got = pl.pallas_call(
            body,
            name=name,
            in_specs=[place(a, k) for k, a in enumerate(args)],
            out_specs=[place(o) for o in outs] + [place(None)] * len(kept),
            out_shape=[typed(o) for o in outs] + [typed(Held(a.array)) for a in kept],
            scratch_shapes=held + [pltpu.VMEM(c, F32) for c in scratch] + sems,
            compiler_params=pltpu.CompilerParams(vmem_limit_bytes=VMEM_LIMIT),
        )(*[placed(a) for a in args])
        return got if isinstance(out_shape, list) or kept else got[0]

    return run


def after(array, other):
    return lax.optimization_barrier((array, other))[0]


def scan_states(total, send, rates, count, place, size, works):
    modes2, width = total.shape
    prefix = ()
    group = 1
    done = []
    for fan, work in zip((2, 4, 4), works):
        others = {d: swapped(send, d * group) for d in (1, 3, 2)[: fan - 1]}
        others = [others[d] for d in range(1, fan)]
        done.append(work and work(send, *done))
        total = after(total, done[-1]) if work else total
        last = group * fan >= size
        outs = [shape(modes2, width, F32)]
        if not last:
            outs += [shape(modes2, width, F32), shape(modes2, width)]

        def kernel(*refs, group=group, fan=fan):
            scan_kernel(count, group, fan, size, refs)

        got = call(kernel, "scan%d" % group, outs, scalars=1)(place, rates, total, *others, *prefix)
        prefix = (got[0],)
        if not last:
            total, send = got[1], got[2]
        group *= fan
    return prefix[0], done


def on_device(
    value, gate_q1, gate_k1, gate_q2, gate_k2, gate_q3, gate_k3, grad_out,
    short_filter, medium_filter, residues, rates,
):
    count, width = value.shape
    modes, groups = rates.shape
    taps, rim = short_filter.shape[0], medium_filter.shape[0]
    ctx, tp, place = axes()
    place = jnp.reshape(place, (1,)).astype(jnp.int32)
    forward, backward = dft_tables(count)
    fwd32 = jnp.asarray(forward[:, :count], F32)
    fwd = jnp.asarray(forward, BF)
    inv = jnp.asarray(backward[:count], BF)
    lag = jnp.asarray(backward[(-np.arange(rim)) % (2 * count)], BF)
    head = count - rim - 16
    value, gate_q1, gate_k1, gate_k2 = [
        Big(a, kept=True, head=head) for a in (value, gate_q1, gate_k1, gate_k2)
    ]
    gate_q2, gate_q3, gate_k3, grad_out = [
        Big(a, kept=True) for a in (gate_q2, gate_q3, gate_k3, grad_out)
    ]
    tables = [Big(t, t.shape[1], kept=True) for t in (fwd32, fwd, inv, lag)]
    full, ext_full = Big(shape(count, width)), (count + 16, width)
    kept, wide = Held(shape(count, width)), Held(shape(count, width, F32))
    filters = Held(jax.ShapeDtypeStruct((3, count, groups), F32))

    def hold(arrays):
        return [Held(a) for a in arrays]

    rim_send, *got = call(
        fore_rim_kernel, "fore_rim", shape(rim + 16, width), (rim + 16, width), scalars=1
    )(place, Big(short_filter, width, kept=True), value, gate_k1, gate_q1, gate_k2)
    short_filter, value, gate_k1, gate_q1, gate_k2 = hold(got)
    rim_fore = shifted(rim_send, 1)
    got = call(medium_filter_kernel, "medium_filter", filters)(
        tables[0], medium_filter, *tables[1:], grad_out, gate_q3, gate_q2, gate_k3
    )
    med, fwd32, fwd, inv, lag, grad_out, gate_q3, gate_q2, gate_k3 = hold(got)
    back_carry = call(back_carry_kernel, "back_carry", shape(modes, width, F32), (count, width))(
        grad_out, gate_q3, rates
    )

    got = call(
        fore_kernel, "fore",
        [kept] * 6 + [shape(2 * modes, width, F32), shape(2 * modes, width)],
        ext_full, (count, width),
    )(value, gate_k1, gate_q1, gate_k2, gate_q2, gate_k3, rim_fore, short_filter, rates, back_carry,
      fwd, inv, med)
    z1, x1, u2, z2, x2, u3 = hold(got[:6])
    carry, send = got[6:]

    def long_side(start, _):
        lng = call(long_filter_kernel, "long_filter", filters, (count, groups))(
            fwd32, residues, after(rates, start)
        )
        return lng, call(back_near_kernel, "back_near", wide)(
            grad_out, gate_q3, fwd, inv, Held(lng)
        )

    def fore_near(start, _, sides):
        return call(fore_near_kernel, "fore_near", wide)(
            u3, fwd, inv, Held(after(sides[0], start))
        )

    states, (_, (lng, du3_near), z3_near) = scan_states(
        carry, send, rates, count, place, ctx, (None, long_side, fore_near)
    )

    du3, dz2, spec, rim_back_send = call(
        back_long_kernel, "back_long",
        [wide, kept, Held(shape(2 * count, width)), shape(rim + 16, width)], (count, width),
    )(Held(du3_near), states, rates, residues, gate_k3, gate_q2, gate_k2, gate_q1, fwd, inv, med)
    dz2 = Held(dz2)
    rim_back = shifted(rim_back_send, -1)
    grad_k3, grad_q2, du2_near = call(back_rest_kernel, "back_rest", [full] * 2 + [wide])(
        Held(du3), Held(spec), x2, z2, gate_k3, inv
    )
    du2_near = Held(du2_near)

    terms = call(medium_terms_kernel, "medium_terms", shape(rim, groups, F32), (2 * count, groups))(
        dz2, u2, rim_fore, fwd, lag
    )
    mixed, grad_q3 = call(fore_long_kernel, "fore_long", [full] * 2, (count, width))(
        Held(z3_near), states, rates, residues, gate_q3, grad_out
    )
    terms = after(terms, mixed)

    packet = (ctx, 8, groups // 2 + LANES)
    grad_k2, grad_q1, grad_k1, grad_value, out = call(
        back_short_kernel, "back_short",
        [full] * 4 + [jax.ShapeDtypeStruct(packet, BF)], ext_full, ext_full, packet,
    )(du2_near, rim_back, x1, z1, gate_k2, gate_q1, gate_k1, value, rim_fore, short_filter, terms,
      fwd, inv, med)

    spread, part = call(
        first_sum_kernel, "first_sum",
        [jax.ShapeDtypeStruct((tp, 8, groups // 2), BF), shape(8, packet[2], F32)],
    )(exchanged(out, "ctx"))
    piece = call(second_sum_kernel, "second_sum", jax.ShapeDtypeStruct(packet, BF))(
        exchanged(spread, "tp"), part
    )
    grad_short, grad_medium = call(
        collect_kernel, "collect", [shape(taps, width, F32), shape(rim, groups, F32)]
    )(exchanged(piece, "ctx"))
    return (
        mixed, grad_value, grad_q1, grad_k1, grad_q2, grad_k2, grad_q3, grad_k3, grad_short, grad_medium,
    )


def solution(mesh):
    data = P("ctx", "tp")
    return jax.shard_map(
        on_device,
        mesh=mesh,
        in_specs=(data,) * 8 + (P(None, "tp"), P(), P(), P()),
        out_specs=(data,) * 8 + (P(None, "tp"), P()),
        check_vma=False,
    )
```

```python
import jax
import jax.numpy as jnp
import numpy as np
from jax import lax
from jax.experimental import pallas as pl
from jax.experimental.pallas import tpu as pltpu
from jax.sharding import PartitionSpec as P

F32 = jnp.float32
BF = jnp.bfloat16
LANES = 128
VMEM_LIMIT = 28 * 1024 * 1024
BLOCK = 256
WIDE = 512
UNROLL = 16
LATE = 99


def dft_tables(count):
    size = 2 * count
    freq = np.arange(count)[:, None].astype(np.int64)

    def waves(times):
        phase = (freq * times[None, :]) % size * (2.0 * np.pi / size)
        cosine, sine = np.cos(phase), -np.sin(phase)
        sine[0] = np.where(times % 2 == 0, 1.0, -1.0)
        return np.concatenate([cosine, sine], axis=0)

    forward = waves(np.arange(size))
    scale = np.full((size, 1), 2.0 / size)
    scale[0] = scale[count] = 1.0 / size
    backward = (forward * scale).T
    return forward, backward


def dot(a, b):
    return jnp.dot(a, b, preferred_element_type=F32)


def spec_mul(spec, filt):
    half = spec.shape[0] // 2
    re, im = spec[:half], spec[half:]
    a, b, c = filt
    return jnp.concatenate([(re * a - im * b).astype(BF), (re * b + im * c).astype(BF)], axis=0)


def spec_conj(spec, filt):
    half = spec.shape[0] // 2
    re, im = spec[:half], spec[half:]
    a, b, c = filt
    return jnp.concatenate([(re * a + im * b).astype(BF), (im * c - re * b).astype(BF)], axis=0)


def row_index(shape):
    return lax.broadcasted_iota(jnp.int32, shape, 0)


def end_states(signal_ref, rates_ref, lanes, own, reverse):
    tiles = signal_ref.shape[0] // 8
    modes = rates_ref.shape[0]
    rates = rates_ref[:, own]
    step = jnp.exp(-8.0 * rates)
    steps = [jnp.broadcast_to(step[m : m + 1], (8, LANES)) for m in range(modes)]

    def body(j, sums):
        tile = tiles - 1 - j if reverse else j
        u = signal_ref[pl.ds(pl.multiple_of(tile * 8, 8), 8), lanes]
        return tuple(s * a + u for s, a in zip(sums, steps))

    zero = jnp.zeros((8, LANES), F32)
    sums = lax.fori_loop(0, tiles, body, (zero,) * modes, unroll=UNROLL)
    sub = row_index((8, LANES)).astype(F32)
    ages = sub if reverse else 7.0 - sub
    rows = [
        jnp.sum(s * jnp.exp(-rates[m : m + 1] * ages), axis=0, keepdims=True)
        for m, s in enumerate(sums)
    ]
    return jnp.concatenate(rows, axis=0)


def far_field(states, rates, weights, out_ref, reverse, first, lanes):
    tiles = out_ref.shape[0] // 8
    modes = rates.shape[0]
    weights = weights * jnp.sqrt(2.0 * rates)
    if states is not None:
        weights = weights * states
    step = jnp.exp(-8.0 * rates)
    steps = [jnp.broadcast_to(step[m : m + 1], (8, LANES)) for m in range(modes)]
    sub = row_index((8, LANES)).astype(F32)
    ages = (7.0 - sub if reverse else sub) + float(first)
    terms = tuple(weights[m : m + 1] * jnp.exp(-rates[m : m + 1] * ages) for m in range(modes))

    def body(j, terms):
        tile = tiles - 1 - j if reverse else j
        level = list(terms)
        while len(level) > 1:
            level = [level[i] + level[i + 1] for i in range(0, len(level), 2)]
        out_ref[pl.ds(pl.multiple_of(tile * 8, 8), 8), lanes] = level[0]
        return tuple(s * a for s, a in zip(terms, steps))

    lax.fori_loop(0, tiles, body, terms, unroll=UNROLL)


def parts(width, groups, size=BLOCK):
    for start in range(0, width, size):
        own = start % groups
        yield slice(start, start + size), slice(own, own + size)


def mul(a, b):
    return a.astype(F32) * b.astype(F32)


def short_causal(ext, filt, rows, start, lanes):
    total = None
    for lag in range(filt.shape[0]):
        term = ext[pl.ds(start - lag, rows), lanes] * filt[lag : lag + 1, lanes].astype(F32)
        total = term if total is None else total + term
    return total


def fore_rim_kernel(
    flow, place_ref, filt_ref, value_ref, k1_ref, q1_ref, k2_ref, out_ref, *refs
):
    ext = refs[-1]
    del place_ref
    count, width = value_ref.shape
    rim = out_ref.shape[0] - 16
    top = count - rim - 16
    for block, (lanes, _) in enumerate(parts(width, width)):
        flow.ready(block)
        u1 = mul(k1_ref[top:, lanes], value_ref[top:, lanes]).astype(BF)
        ext[:, lanes] = u1.astype(F32)
        z1 = short_causal(ext, filt_ref, rim, 16, lanes)
        x1 = mul(q1_ref[count - rim :, lanes], z1).astype(BF)
        out_ref[0:rim, lanes] = mul(k2_ref[count - rim :, lanes], x1).astype(BF)
        out_ref[rim : rim + 16, lanes] = u1[rim:]


def spectrum(table, filt, out):
    count = out.shape[1]
    spec = jnp.dot(
        table[:, : filt.shape[0]], filt, precision=lax.Precision.HIGHEST, preferred_element_type=F32
    )
    re, im = spec[:count], spec[count:]
    edge = row_index(re.shape) == 0
    out[0] = re
    out[1] = jnp.where(edge, 0.0, im)
    out[2] = jnp.where(edge, im, re)


def medium_filter_kernel(flow, table_ref, medium_ref, *refs):
    out_ref = refs[-1]
    flow.ready(0)
    spectrum(table_ref, medium_ref[...].astype(F32), out_ref)
    for piece in range(1, 4):
        flow.ready(piece)


def long_filter_kernel(table_ref, residues_ref, rates_ref, out_ref, local):
    for lanes, _ in parts(local.shape[1], local.shape[1], LANES):
        far_field(None, rates_ref[:, lanes], residues_ref[:, lanes], local, False, 0, lanes)
    spectrum(table_ref, local[...], out_ref)


def filt_of(ref, own):
    return ref[0, :, own], ref[1, :, own], ref[2, :, own]


def back_carry_kernel(grad_ref, gate_ref, rates_ref, carry_ref, signal):
    count, width = grad_ref.shape
    groups = rates_ref.shape[1]
    for lanes, own in parts(width, groups):
        signal[:, lanes] = mul(grad_ref[:, lanes], gate_ref[:, lanes])
        for side in range(0, BLOCK, LANES):
            at = slice(lanes.start + side, lanes.start + side + LANES)
            mine = slice(own.start + side, own.start + side + LANES)
            carry_ref[:, at] = end_states(signal, rates_ref, at, mine, True)


def back_near_kernel(grad_ref, gate_ref, fwd_ref, inv_ref, long_ref, near_ref):
    count, width = grad_ref.shape
    for lanes, own in parts(width, long_ref.shape[2]):
        spec = dot(fwd_ref[:, :count], mul(grad_ref[:, lanes], gate_ref[:, lanes]).astype(BF))
        near_ref[:, lanes] = dot(inv_ref[...], spec_conj(spec, filt_of(long_ref, own)))


def fore_start_kernel(value_ref, k1_ref, q1_ref, k2_ref, filt_ref, z1_ref, x1_ref, u2_ref, ext):
    count, width = value_ref.shape
    for lanes, _ in parts(width, width, WIDE):
        ext[:, lanes] = mul(k1_ref[:, lanes], value_ref[:, lanes]).astype(BF).astype(F32)
        z1 = short_causal(ext, filt_ref, count - 16, 16, lanes)
        z1_ref[16:, lanes] = z1.astype(BF)
        x1 = mul(q1_ref[16:, lanes], z1).astype(BF)
        x1_ref[16:, lanes] = x1
        u2_ref[16:, lanes] = mul(k2_ref[16:, lanes], x1).astype(BF)


def fore_kernel(
    value_ref, k1_ref, q1_ref, k2_ref, q2_ref, k3_ref, rim_ref, filt_ref, rates_ref, back_ref,
    z1_in, x1_in, u2_in, fwd_ref, inv_ref, med_ref,
    z1_ref, x1_ref, u2_ref, z2_ref, x2_ref, u3_ref, carry_ref, send_ref, ext, signal,
):
    count, width = value_ref.shape
    modes, groups = rates_ref.shape
    rim = rim_ref.shape[0] - 16
    for lanes, own in parts(width, groups, WIDE):
        u1 = mul(k1_ref[0:16, lanes], value_ref[0:16, lanes]).astype(BF)
        ext[0:16, lanes] = rim_ref[rim : rim + 16, lanes].astype(F32)
        ext[16:32, lanes] = u1.astype(F32)
        z1 = short_causal(ext, filt_ref, 16, 16, lanes)
        z1_ref[0:16, lanes] = z1.astype(BF)
        z1_ref[16:, lanes] = z1_in[16:, lanes]
        x1 = mul(q1_ref[0:16, lanes], z1).astype(BF)
        x1_ref[0:16, lanes] = x1
        x1_ref[16:, lanes] = x1_in[16:, lanes]
        u2 = mul(k2_ref[0:16, lanes], x1).astype(BF)
        u2 = jnp.concatenate([u2, u2_in[16:, lanes]], axis=0)
        u2_ref[:, lanes] = u2
        spec = dot(fwd_ref[:, :count], u2)
        spec = spec + dot(fwd_ref[:, 2 * count - rim :], rim_ref[0:rim, lanes])
        z2 = dot(inv_ref[...], spec_mul(spec, filt_of(med_ref, own)))
        z2_ref[:, lanes] = z2.astype(BF)
        x2 = mul(q2_ref[:, lanes], z2).astype(BF)
        x2_ref[:, lanes] = x2
        u3 = mul(k3_ref[:, lanes], x2).astype(BF)
        u3_ref[:, lanes] = u3
        signal[:, lanes] = u3.astype(F32)
    carry_ref[0:modes, :] = back_ref[...]
    for lanes, own in parts(width, groups, LANES):
        carry_ref[modes:, lanes] = end_states(signal, rates_ref, lanes, own, False)
    send_ref[...] = carry_ref[...].astype(BF)


def back_long_kernel(
    near_ref, state_ref, rates_ref, residues_ref, k3_ref, q2_ref, k2_ref, q1_ref,
    fwd_ref, inv_ref, med_ref,
    du3_ref, dz2_ref, spec_ref, rim_ref, far,
):
    count, width = near_ref.shape
    modes, groups = rates_ref.shape
    rim = rim_ref.shape[0] - 16
    for lanes, own in parts(width, groups, LANES):
        far_field(
            state_ref[0:modes, lanes], rates_ref[:, own], residues_ref[:, own], far, True, 1, lanes
        )
    for lanes, own in parts(width, groups, WIDE):
        du3 = near_ref[:, lanes] + far[:, lanes]
        du3_ref[:, lanes] = du3
        dx2 = mul(du3, k3_ref[:, lanes]).astype(BF)
        dz2 = mul(dx2, q2_ref[:, lanes]).astype(BF)
        dz2_ref[:, lanes] = dz2
        spec = spec_conj(dot(fwd_ref[:, :count], dz2), filt_of(med_ref, own))
        spec_ref[:, lanes] = spec
        rim_ref[0:rim, lanes] = dz2[0:rim]
        dx1 = mul(dot(inv_ref[0:16, :], spec), k2_ref[0:16, lanes]).astype(BF)
        rim_ref[rim : rim + 16, lanes] = mul(dx1, q1_ref[0:16, lanes]).astype(BF)


def back_rest_kernel(
    flow, du3_ref, spec_ref, x2_ref, z2_ref, k3_ref, inv_ref, gk3_ref, gq2_ref, du2_ref
):
    width = du3_ref.shape[1]
    for block, (lanes, _) in enumerate(parts(width, width)):
        du2_ref[:, lanes] = dot(inv_ref[...], spec_ref[:, lanes])
        du3 = du3_ref[:, lanes]
        gk3_ref[:, lanes] = mul(du3, x2_ref[:, lanes]).astype(BF)
        dx2 = mul(du3, k3_ref[:, lanes]).astype(BF)
        gq2_ref[:, lanes] = mul(dx2, z2_ref[:, lanes]).astype(BF)
        flow.flush(block)


def medium_terms_kernel(dz2_ref, u2_ref, rim_ref, fwd_ref, lag_ref, out_ref, total):
    count, width = dz2_ref.shape
    groups = out_ref.shape[1]
    rim = rim_ref.shape[0] - 16
    for lanes, own in parts(width, groups):
        ext = dot(fwd_ref[:, :count], u2_ref[:, lanes])
        ext = ext + dot(fwd_ref[:, 2 * count - rim :], rim_ref[0:rim, lanes])
        grad = dot(fwd_ref[:, :count], dz2_ref[:, lanes])
        er, ei, dr, di = ext[:count], ext[count:], grad[:count], grad[count:]
        edge = row_index(er.shape) == 0
        high = di * ei
        re = dr * er + jnp.where(edge, 0.0, high)
        im = jnp.where(edge, high, dr * ei - di * er)
        if lanes == own:
            total[:count, own] = re
            total[count:, own] = im
        else:
            total[:count, own] += re
            total[count:, own] += im
    out_ref[...] = dot(lag_ref[...], total[...].astype(BF))


def back_short_kernel(
    flow, du2_ref, rim_ref, x1_ref, z1_ref, k2_ref, q1_ref, k1_ref, value_ref, fore_ref, filt_ref,
    terms_ref, fwd_ref, inv_ref, med_ref,
    gk2_ref, gq1_ref, gk1_ref, gv_ref, send_ref, ext, signal, packet,
):
    count, width = du2_ref.shape
    groups = terms_ref.shape[1]
    rim = rim_ref.shape[0] - 16
    taps = filt_ref.shape[0]
    pieces = send_ref.shape[0]
    share = terms_ref.shape[0] // pieces
    half = groups // 2
    packet[...] = jnp.zeros_like(packet)
    for piece in range(pieces):
        rows = terms_ref[piece * share : (piece + 1) * share, :]
        packet[piece, 0:share, 0:half] = rows[:, :half]
        packet[piece, share : 2 * share, 0:half] = rows[:, half:]
    for block, (lanes, own) in enumerate(parts(width, groups)):
        spec = dot(fwd_ref[:, count : count + rim], rim_ref[0:rim, lanes])
        du2 = du2_ref[:, lanes] + dot(inv_ref[...], spec_conj(spec, filt_of(med_ref, own)))
        gk2_ref[:, lanes] = mul(du2, x1_ref[:, lanes]).astype(BF)
        dx1 = mul(du2, k2_ref[:, lanes]).astype(BF)
        gq1_ref[:, lanes] = mul(dx1, z1_ref[:, lanes]).astype(BF)
        dz1 = mul(dx1, q1_ref[:, lanes]).astype(BF).astype(F32)
        ext[0:count, lanes] = dz1
        ext[count:, lanes] = rim_ref[rim : rim + 16, lanes].astype(F32)
        signal[0:16, lanes] = fore_ref[rim : rim + 16, lanes].astype(F32)
        signal[16:, lanes] = mul(k1_ref[:, lanes], value_ref[:, lanes]).astype(BF).astype(F32)
        du1 = None
        for lag in range(taps):
            term = ext[pl.ds(lag, count), lanes] * filt_ref[lag : lag + 1, lanes].astype(F32)
            du1 = term if du1 is None else du1 + term
        gk1_ref[:, lanes] = mul(du1, value_ref[:, lanes]).astype(BF)
        gv_ref[:, lanes] = mul(du1, k1_ref[:, lanes]).astype(BF)
        flow.flush(block)
        for lag in range(taps):
            row = jnp.sum(dz1 * signal[pl.ds(16 - lag, count), lanes], axis=0, keepdims=True)
            spot = lag * (width // BLOCK) + block
            packet[spot, 0:1, half : half + LANES] = row[:, :LANES]
            packet[spot, 1:2, half : half + LANES] = row[:, LANES:]
    send_ref[...] = packet[...].astype(send_ref.dtype)


def fore_near_kernel(u3_ref, fwd_ref, inv_ref, long_ref, near_ref):
    count, width = u3_ref.shape
    for lanes, own in parts(width, long_ref.shape[2]):
        spec = dot(fwd_ref[:, :count], u3_ref[:, lanes])
        near_ref[:, lanes] = dot(inv_ref[...], spec_mul(spec, filt_of(long_ref, own)))


def fore_long_kernel(
    flow, near_ref, state_ref, rates_ref, residues_ref, q3_ref, grad_ref, mixed_ref, gq3_ref, far
):
    width = near_ref.shape[1]
    modes, groups = rates_ref.shape
    for block, (lanes, own) in enumerate(parts(width, groups)):
        for side in range(0, BLOCK, LANES):
            at = slice(lanes.start + side, lanes.start + side + LANES)
            mine = slice(own.start + side, own.start + side + LANES)
            far_field(
                state_ref[modes:, at], rates_ref[:, mine], residues_ref[:, mine], far, False, 1, at
            )
        z3 = far[:, lanes] + near_ref[:, lanes]
        mixed_ref[:, lanes] = mul(q3_ref[:, lanes], z3).astype(BF)
        gq3_ref[:, lanes] = mul(grad_ref[:, lanes], z3).astype(BF)
        flow.flush(block)


def scan_kernel(count, group, fan, size, refs):
    place_ref, rates_ref, total_ref = refs[:3]
    others = refs[3 : 2 + fan]
    rest = refs[2 + fan :]
    prefix_ref = None if group == 1 else rest[0]
    outs = rest if group == 1 else rest[1:]
    modes, groups = rates_ref.shape
    width = total_ref.shape[1]
    place = place_ref[0]
    last = group * fan >= size
    for side in range(2):
        rows = slice(side * modes, (side + 1) * modes)
        at = size - 1 - place if side == 0 else place
        mine = (at // group) % fan
        offset = at % group
        drop = rates_ref[...] * float(-count)

        def power(n, keep=None):
            value = jnp.exp(drop * n.astype(F32))
            return value if keep is None else jnp.where(keep, value, 0.0)

        for copy in range(width // groups):
            lanes = slice(copy * groups, (copy + 1) * groups)
            prefix = jnp.zeros((modes, groups), F32) if group == 1 else prefix_ref[rows, lanes]
            total = None
            if not last:
                total = total_ref[rows, lanes] * power(group * (fan - 1 - mine))
            for d, other in enumerate(others, 1):
                theirs = mine ^ d
                before = theirs < mine
                block = other[rows, lanes].astype(F32)
                gap = jnp.where(before, offset + group * (mine - 1 - theirs), 0)
                prefix = prefix + power(gap, before) * block
                if not last:
                    total = total + power(group * (fan - 1 - theirs)) * block
            outs[0][rows, lanes] = prefix
            if not last:
                outs[1][rows, lanes] = total
                outs[2][rows, lanes] = total.astype(BF)


def first_sum_kernel(got_ref, spread_ref, part_ref):
    part = jnp.sum(got_ref[...].astype(F32), axis=0)
    part_ref[...] = part
    half = spread_ref.shape[2]
    spread_ref[...] = jnp.broadcast_to(part[None, :, :half], spread_ref.shape).astype(
        spread_ref.dtype
    )


def second_sum_kernel(got_ref, part_ref, piece_ref):
    medium = jnp.sum(got_ref[...].astype(F32), axis=0)
    half = medium.shape[1]
    piece = jnp.concatenate([medium, part_ref[:, half:]], axis=1)
    piece_ref[...] = jnp.broadcast_to(piece[None], piece_ref.shape).astype(piece_ref.dtype)


def collect_kernel(full_ref, short_ref, medium_ref):
    pieces = full_ref.shape[0]
    half = medium_ref.shape[1] // 2
    share = medium_ref.shape[0] // pieces
    for piece in range(pieces):
        rows = full_ref[piece].astype(F32)
        place = slice(piece * share, (piece + 1) * share)
        medium_ref[place, :half] = rows[0:share, :half]
        medium_ref[place, half:] = rows[share : 2 * share, :half]
    blocks = short_ref.shape[1] // BLOCK
    for lag in range(short_ref.shape[0]):
        for block in range(blocks):
            rows = full_ref[lag * blocks + block].astype(F32)
            for side in range(2):
                start = block * BLOCK + side * LANES
                short_ref[lag : lag + 1, start : start + LANES] = rows[side : side + 1, half:]


def swapped(block, distance):
    size = lax.axis_size("ctx")
    return lax.ppermute(block, "ctx", [(i, i ^ distance) for i in range(size)])


def shifted(block, distance):
    size = lax.axis_size("ctx")
    route = [(i, i + distance) for i in range(size) if 0 <= i + distance < size]
    return lax.ppermute(block, "ctx", route)


def exchanged(block, axis):
    return lax.all_to_all(block, axis, 0, 0)


def axes():
    return lax.axis_size("ctx"), lax.axis_size("tp"), lax.axis_index("ctx")


def shape(rows, cols, dtype=BF):
    return jax.ShapeDtypeStruct((rows, cols), dtype)


class Big:
    def __init__(self, array, block=BLOCK, kept=False, head=0):
        self.array, self.block, self.kept, self.head = array, block, kept, head

    def count(self):
        return len(self.lanes()) * (2 if self.head else 1)

    def boxes(self, piece):
        lead = (slice(None),) * (len(self.array.shape) - 1)
        lanes = (self.lanes()[piece],)
        if not self.head:
            return [(piece, lead + lanes)]
        top = (slice(0, self.head),) + lanes
        return [(piece, (slice(self.head, self.array.shape[0]),) + lanes), (LATE, top)]

    def lanes(self):
        width = self.array.shape[-1]
        return [slice(k, k + self.block) for k in range(0, width, self.block)]


class Held:
    def __init__(self, array):
        self.array = array


class Moves:
    def __init__(self, sources, targets, arrays, sems):
        self.copies, count = {}, 0
        for piece in range(max([len(a.lanes()) for a in arrays], default=0)):
            for source, target, array in zip(sources, targets, arrays):
                if piece < len(array.lanes()):
                    for key, at in array.boxes(piece):
                        copy = pltpu.make_async_copy(source.at[at], target.at[at], sems.at[count])
                        self.copies.setdefault(key, []).append(copy)
                        count += 1

    def start(self, piece):
        for copy in self.copies.get(piece, []):
            copy.start()

    def wait(self, piece):
        for copy in self.copies.get(piece, []):
            copy.wait()


class Flow:
    def __init__(self, loads, stores):
        self.loads, self.stores = loads, stores
        for piece in sorted(loads.copies):
            loads.start(piece)

    def ready(self, piece):
        self.loads.wait(piece)

    def flush(self, piece):
        self.stores.start(piece)


def call(kernel, name, out_shape, *scratch, scalars=0):
    outs = out_shape if isinstance(out_shape, list) else [out_shape]

    def typed(o):
        if isinstance(o, Big):
            return pltpu.HBM(o.array.shape, o.array.dtype)
        return pltpu.VMEM(o.array.shape, o.array.dtype) if isinstance(o, Held) else o

    def placed(a):
        if isinstance(a, Big):
            return pltpu.with_memory_space_constraint(a.array, pltpu.HBM)
        if isinstance(a, Held):
            return pltpu.with_memory_space_constraint(a.array, pltpu.VMEM)
        return a

    def run(*args):
        big_in = [a for a in args if isinstance(a, Big)]
        kept = [a for a in big_in if a.kept]
        big_out = [o for o in outs if isinstance(o, Big)]

        def body(*refs):
            ins, rest = list(refs[: len(args)]), refs[len(args) :]
            results, rest = list(rest[: len(outs)]), rest[len(outs) :]
            held_kept, rest = iter(rest[: len(kept)]), rest[len(kept) :]
            fresh = len(big_in) - len(kept)
            held_new, rest = iter(rest[:fresh]), rest[fresh:]
            held_in = [next(held_kept) if a.kept else next(held_new) for a in big_in]
            held_out, rest = rest[: len(big_out)], rest[len(big_out) :]
            own, sems = rest[: len(scratch)], rest[len(scratch) :]
            if not big_in and not big_out:
                kernel(*ins, *results, *own)
                return
            at_in = [k for k, a in enumerate(args) if isinstance(a, Big)]
            at_out = [k for k, o in enumerate(outs) if isinstance(o, Big)]
            loads = Moves([ins[k] for k in at_in], held_in, big_in, sems[0])
            stores = Moves(held_out, [results[k] for k in at_out], big_out, sems[1])
            for k, ref in zip(at_in, held_in):
                ins[k] = ref
            for k, ref in zip(at_out, held_out):
                results[k] = ref
            kernel(Flow(loads, stores), *ins, *results, *own)
            loads.wait(LATE)
            for piece in stores.copies:
                stores.wait(piece)

        def place(a, k=None):
            if isinstance(a, Big):
                return pl.BlockSpec(memory_space=pltpu.HBM)
            return pl.BlockSpec(memory_space=pltpu.SMEM if k is not None and k < scalars else pltpu.VMEM)

        held = [pltpu.VMEM(a.array.shape, a.array.dtype) for a in big_in + big_out if not a.kept]
        sems = []
        if big_in or big_out:
            for group in (big_in, big_out):
                sems.append(pltpu.SemaphoreType.DMA((max(1, sum(a.count() for a in group)),)))
        got = pl.pallas_call(
            body,
            name=name,
            in_specs=[place(a, k) for k, a in enumerate(args)],
            out_specs=[place(o) for o in outs] + [place(None)] * len(kept),
            out_shape=[typed(o) for o in outs] + [typed(Held(a.array)) for a in kept],
            scratch_shapes=held + [pltpu.VMEM(c, F32) for c in scratch] + sems,
            compiler_params=pltpu.CompilerParams(vmem_limit_bytes=VMEM_LIMIT),
        )(*[placed(a) for a in args])
        return got if isinstance(out_shape, list) or kept else got[0]

    return run


def after(array, other):
    return lax.optimization_barrier((array, other))[0]


def scan_states(total, send, rates, count, place, size, works):
    modes2, width = total.shape
    prefix = ()
    group = 1
    done = []
    for fan, work in zip((2, 4, 4), works):
        others = {d: swapped(send, d * group) for d in (1, 3, 2)[: fan - 1]}
        others = [others[d] for d in range(1, fan)]
        done.append(work and work(send, *done))
        total = after(total, done[-1]) if work else total
        last = group * fan >= size
        outs = [shape(modes2, width, F32)]
        if not last:
            outs += [shape(modes2, width, F32), shape(modes2, width)]

        def kernel(*refs, group=group, fan=fan):
            scan_kernel(count, group, fan, size, refs)

        got = call(kernel, "scan%d" % group, outs, scalars=1)(place, rates, total, *others, *prefix)
        prefix = (got[0],)
        if not last:
            total, send = got[1], got[2]
        group *= fan
    return prefix[0], done


def on_device(
    value, gate_q1, gate_k1, gate_q2, gate_k2, gate_q3, gate_k3, grad_out,
    short_filter, medium_filter, residues, rates,
):
    count, width = value.shape
    modes, groups = rates.shape
    taps, rim = short_filter.shape[0], medium_filter.shape[0]
    ctx, tp, place = axes()
    place = jnp.reshape(place, (1,)).astype(jnp.int32)
    forward, backward = dft_tables(count)
    fwd32 = jnp.asarray(forward[:, :count], F32)
    fwd = jnp.asarray(forward, BF)
    inv = jnp.asarray(backward[:count], BF)
    lag = jnp.asarray(backward[(-np.arange(rim)) % (2 * count)], BF)
    head = count - rim - 16
    value, gate_q1, gate_k1, gate_k2 = [
        Big(a, kept=True, head=head) for a in (value, gate_q1, gate_k1, gate_k2)
    ]
    gate_q2, gate_q3, gate_k3, grad_out = [
        Big(a, kept=True) for a in (gate_q2, gate_q3, gate_k3, grad_out)
    ]
    tables = [Big(t, t.shape[1], kept=True) for t in (fwd32, fwd, inv, lag)]
    full, ext_full = Big(shape(count, width)), (count + 16, width)
    kept, wide = Held(shape(count, width)), Held(shape(count, width, F32))
    filters = Held(jax.ShapeDtypeStruct((3, count, groups), F32))

    def hold(arrays):
        return [Held(a) for a in arrays]

    rim_send, *got = call(
        fore_rim_kernel, "fore_rim", shape(rim + 16, width), (rim + 16, width), scalars=1
    )(place, Big(short_filter, width, kept=True), value, gate_k1, gate_q1, gate_k2)
    short_filter, value, gate_k1, gate_q1, gate_k2 = hold(got)
    rim_fore = shifted(rim_send, 1)
    got = call(medium_filter_kernel, "medium_filter", filters)(
        tables[0], medium_filter, *tables[1:], grad_out, gate_q3, gate_q2, gate_k3
    )
    med, fwd32, fwd, inv, lag, grad_out, gate_q3, gate_q2, gate_k3 = hold(got)
    back_carry = call(back_carry_kernel, "back_carry", shape(modes, width, F32), (count, width))(
        grad_out, gate_q3, rates
    )

    begun = call(fore_start_kernel, "fore_start", [kept] * 3, (count, width))(
        value, gate_k1, gate_q1, gate_k2, short_filter
    )
    got = call(
        fore_kernel, "fore",
        [kept] * 6 + [shape(2 * modes, width, F32), shape(2 * modes, width)],
        (32, width), (count, width),
    )(value, gate_k1, gate_q1, gate_k2, gate_q2, gate_k3, rim_fore, short_filter, rates, back_carry,
      *hold(begun), fwd, inv, med)
    z1, x1, u2, z2, x2, u3 = hold(got[:6])
    carry, send = got[6:]

    def long_side(start, _):
        lng = call(long_filter_kernel, "long_filter", filters, (count, groups))(
            fwd32, residues, after(rates, start)
        )
        return lng, call(back_near_kernel, "back_near", wide)(
            grad_out, gate_q3, fwd, inv, Held(lng)
        )

    def fore_near(start, _, sides):
        return call(fore_near_kernel, "fore_near", wide)(
            u3, fwd, inv, Held(after(sides[0], start))
        )

    states, (_, (lng, du3_near), z3_near) = scan_states(
        carry, send, rates, count, place, ctx, (None, long_side, fore_near)
    )

    du3, dz2, spec, rim_back_send = call(
        back_long_kernel, "back_long",
        [wide, kept, Held(shape(2 * count, width)), shape(rim + 16, width)], (count, width),
    )(Held(du3_near), states, rates, residues, gate_k3, gate_q2, gate_k2, gate_q1, fwd, inv, med)
    dz2 = Held(dz2)
    rim_back = shifted(rim_back_send, -1)
    grad_k3, grad_q2, du2_near = call(back_rest_kernel, "back_rest", [full] * 2 + [wide])(
        Held(du3), Held(spec), x2, z2, gate_k3, inv
    )
    du2_near = Held(du2_near)

    terms = call(medium_terms_kernel, "medium_terms", shape(rim, groups, F32), (2 * count, groups))(
        dz2, u2, rim_fore, fwd, lag
    )
    mixed, grad_q3 = call(fore_long_kernel, "fore_long", [full] * 2, (count, width))(
        Held(z3_near), states, rates, residues, gate_q3, grad_out
    )
    terms = after(terms, mixed)

    packet = (ctx, 8, groups // 2 + LANES)
    grad_k2, grad_q1, grad_k1, grad_value, out = call(
        back_short_kernel, "back_short",
        [full] * 4 + [jax.ShapeDtypeStruct(packet, BF)], ext_full, ext_full, packet,
    )(du2_near, rim_back, x1, z1, gate_k2, gate_q1, gate_k1, value, rim_fore, short_filter, terms,
      fwd, inv, med)

    spread, part = call(
        first_sum_kernel, "first_sum",
        [jax.ShapeDtypeStruct((tp, 8, groups // 2), BF), shape(8, packet[2], F32)],
    )(exchanged(out, "ctx"))
    piece = call(second_sum_kernel, "second_sum", jax.ShapeDtypeStruct(packet, BF))(
        exchanged(spread, "tp"), part
    )
    grad_short, grad_medium = call(
        collect_kernel, "collect", [shape(taps, width, F32), shape(rim, groups, F32)]
    )(exchanged(piece, "ctx"))
    return (
        mixed, grad_value, grad_q1, grad_k1, grad_q2, grad_k2, grad_q3, grad_k3, grad_short, grad_medium,
    )


def solution(mesh):
    data = P("ctx", "tp")
    return jax.shard_map(
        on_device,
        mesh=mesh,
        in_specs=(data,) * 8 + (P(None, "tp"), P(), P(), P()),
        out_specs=(data,) * 8 + (P(None, "tp"), P()),
        check_vma=False,
    )
```
